32 devices in a mesh: grp: 2 (over x), gs: 16 (over z, y, core).
Axes of the slice: x: 2, y: 2, z: 4, core: 2. Of those that a mesh axis runs over, the one named last changes fastest.
Arguments:
- centres: float32 [3, 131072], P(None, ('grp', 'gs')), parts along dimension 1, may hold values from -6 to 7, as said below
- factor: float32 [9, 131072], P(None, ('grp', 'gs')), parts along dimension 1, may hold values from -0.048 to 0.048
- harmonics: float32 [48, 131072], P(None, ('grp', 'gs')), parts along dimension 1, may hold values from -3.6 to 3.6
- opacity: float32 [131072], P(('grp', 'gs')), parts along dimension 0, may hold values from -4 to 0
- cameras: float32 [8, 3], P('grp'), parts along dimension 0, may hold values from -0.5 to 0.5, as said below
- requests: int32 [16384], P(('grp', 'gs')), parts along dimension 0, may hold values from -1 to 4095, as said below
- tile_lists: int32 [256, 512], P(('grp', 'gs')), parts along dimension 0, may hold values from -1 to 511, as said below
- tile_ids: int32 [256], P(('grp', 'gs')), parts along dimension 0, may hold values from 0 to 7919, as said below
- image_cotangent: float32 [3, 256, 256], P(None, ('grp', 'gs')), parts along dimension 1, may hold values from -6 to 6
Outputs:
- image: float32 [3, 256, 256], P(None, ('grp', 'gs')), parts along dimension 1
- grad_centres: float32 [3, 131072], P(None, ('grp', 'gs')), parts along dimension 1
- grad_factor: float32 [9, 131072], P(None, ('grp', 'gs')), parts along dimension 1
- grad_harmonics: float32 [48, 131072], P(None, ('grp', 'gs')), parts along dimension 1
- grad_opacity: float32 [131072], P(('grp', 'gs')), parts along dimension 0
The draws below stay inside these ranges and needn't reach their ends.
There are 2 independent parts, one for each index of `grp`. The reference program is written for one: setup_inputs(seed, part) draws one part's arguments, and reference() takes and returns one part's arrays. A program takes and returns all parts, laid end to end along the dimension named above; each array names one. Nothing has to cross between parts.
Inputs may be any that keep to these rules, and one draw needn't show every extreme that they name: `requests`: entry 512 * d + 32 * s + k names the k-th Gaussian (an index among owner s's 4096) that device d asks of owner s, or is -1; the named entries of each pair (d, s) come first. `tile_lists`: row t belongs to device t // 8; an entry r >= 0 names slot r mod 32 of owner r // 32 of that device's requests, and that request is not -1. Entries are in compositing order, front first; after the listed entries a row holds -1 to its end. `tile_ids`: distinct numbers; number v * 60 * 33 + 60 * y + x is tile column x, tile row y of view v. `cameras`: third coordinates lie within 0.25 of zero. `centres`: every centre's third coordinate exceeds every camera's third coordinate by 2.5 or more.
All inputs are finite; a program needn't handle non-finite values.
Results may differ from the reference program's by a relative error of at most 0.0003.
Values sent between devices are 32-bit elements; how exact they have to be, the bound alone decides.
A program may use at most 64 MiB of HBM per device.

```python
import jax
import jax.numpy as jnp
from jax import lax

G_DEV = 4096
TILE_DEV = 8
CAP = 32
LIST = 512
TILE = 16
VIEWS = 4
IMG_W = 960
IMG_H = 540
FOCAL = 600
HARMONICS = 48
PIX = 256
TILES_ACROSS = 60
TILE_ROWS = 33
G = 65536
TILES = 128
SLOTS = 512
N_GS = 16


def camera_draw(key):
    camera_key = jax.random.fold_in(key, 11)
    position = jax.random.uniform(camera_key, (VIEWS, 3), jnp.float32, -0.5, 0.5)
    return position * jnp.array([1.0, 1.0, 0.5], jnp.float32)


def move_front(codes, value, place):
    found = jnp.argmax(codes == value).astype(jnp.int32)
    current = codes[place]
    return codes.at[place].set(codes[found]).at[found].set(current)


def plan_draw(key):
    subkeys = jax.random.split(jax.random.fold_in(key, 23), 8)
    device_count = SLOTS // CAP
    counts = jax.random.randint(subkeys[0], (device_count, device_count), 1, CAP + 1)
    busiest = jax.random.randint(subkeys[1], (), 0, device_count)
    rows_idx = jnp.arange(device_count)
    counts = jnp.where(rows_idx[:, None] == busiest, CAP, counts)
    counts = counts.at[(busiest + 1) % device_count, 0].set(1)
    wanted = jax.random.randint(subkeys[2], (device_count, device_count, CAP), 0, G_DEV)
    wanted = wanted.at[busiest, 0, 0].set(G_DEV - 1)
    filled = jnp.arange(CAP)[None, None, :] < counts[:, :, None]
    requests = jnp.where(filled, wanted, -1).reshape(device_count * SLOTS).astype(jnp.int32)
    tile_total = VIEWS * TILES_ACROSS * TILE_ROWS
    shuffled = jax.random.permutation(subkeys[3], tile_total).astype(jnp.int32)
    shuffled = move_front(shuffled, 0, 0)
    shuffled = move_front(shuffled, tile_total - 1, 1)
    tile_codes = shuffled[:TILES].astype(jnp.int32)
    lengths = jax.random.randint(subkeys[4], (TILES,), LIST // 2, LIST + 1)
    longest = jax.random.randint(subkeys[5], (), 0, TILES)
    lengths = jnp.where(jnp.arange(TILES) == longest, LIST, lengths)
    holder = jnp.arange(TILES) // TILE_DEV
    source_rows = jax.random.randint(subkeys[6], (TILES, LIST), 0, device_count)
    draw_slot = jax.random.randint(subkeys[7], (TILES, LIST), 0, 1 << 20)
    available = counts[holder[:, None], source_rows]
    buffer_row = source_rows * CAP + draw_slot % available
    list_rows = jnp.where(jnp.arange(LIST)[None, :] < lengths[:, None], buffer_row, -1)
    list_rows = list_rows.at[busiest * TILE_DEV, 0].set(SLOTS - 1).astype(jnp.int32)
    return (requests, list_rows, tile_codes)


def draw_requests(key, part):
    return plan_draw(key)[0]


def draw_tile_lists(key, part):
    return plan_draw(key)[1]


def draw_tile_ids(key, part):
    return plan_draw(key)[2]


def draw_cameras(key, part):
    return camera_draw(key)


def draw_centres(key, part):
    requests, list_rows, tile_codes = plan_draw(key)
    camera_pos = camera_draw(key)
    key = jax.random.fold_in(key, 5)
    subkeys = jax.random.split(key, 4)
    device_count = SLOTS // CAP
    holder = jnp.arange(TILES) // TILE_DEV
    listed = list_rows >= 0
    lookup = jnp.where(listed, list_rows, 0)
    local = requests.reshape(device_count, SLOTS)[holder[:, None], lookup]
    global_id = lookup // CAP * G_DEV + local
    entry_code = jnp.arange(TILES)[:, None] * LIST + jnp.arange(LIST)[None, :] + 1
    entry_code = jnp.where(listed, entry_code, 0)
    leading_entry = jnp.zeros((G,), jnp.int32).at[global_id.reshape(-1)].max(entry_code.reshape(-1).astype(jnp.int32))
    placed = leading_entry > 0
    chosen = jnp.maximum(leading_entry - 1, 0)
    tile_row = chosen // LIST
    depth_rank = (chosen % LIST).astype(jnp.float32)
    free_code = jax.random.randint(subkeys[0], (G,), 0, VIEWS * TILES_ACROSS * TILE_ROWS)
    code_now = jnp.where(placed, tile_codes[tile_row], free_code)
    per_view = TILES_ACROSS * TILE_ROWS
    view_idx = code_now // per_view
    remainder = code_now % per_view
    tile_col = (remainder % TILES_ACROSS).astype(jnp.float32)
    tile_line = (remainder // TILES_ACROSS).astype(jnp.float32)
    offsets = jax.random.uniform(subkeys[1], (2, G), jnp.float32, 0.0, 1.0) * TILE
    screen_u = tile_col * TILE + offsets[0]
    screen_w = tile_line * TILE + offsets[1]
    jitter = jax.random.uniform(subkeys[2], (G,), jnp.float32, 0.0, 0.05)
    depth_free = jax.random.uniform(subkeys[3], (G,), jnp.float32, 3.0, 6.0)
    depth = jnp.where(placed, 3.0 + 3.0 * depth_rank / LIST + jitter, depth_free)
    centre = camera_pos[view_idx]
    world_x = centre[:, 0] + depth * (screen_u - 0.5 * IMG_W) / FOCAL
    world_y = centre[:, 1] + depth * (screen_w - 0.5 * IMG_H) / FOCAL
    world_z = centre[:, 2] + depth
    return jnp.stack([world_x, world_y, world_z]).astype(jnp.float32)


def block_scale(key, dims, shards, smallest, top_value):
    def one(dim, shards_of):
        heights = jax.random.uniform(jax.random.fold_in(jax.random.fold_in(key, 6), dim), (shards_of,), jnp.float32, smallest / len(shards), top_value / len(shards))
        return jnp.repeat(jnp.exp(heights), dims[dim] // shards_of).reshape((-1,) + (1,) * (len(dims) - dim - 1))

    level = one(*shards[0])
    for cut in shards[1:]:
        level = level * one(*cut)
    return level


def scatter_about(rng, dims, deviation, most, shards=(), kind=jnp.bfloat16):
    level = block_scale(rng, dims, shards, -0.22, 0.18) if shards else 1.0
    values = jax.random.normal(rng, dims, jnp.float32) * deviation * level
    return jnp.minimum(jnp.maximum(values, -most), most).astype(kind)


def setup_inputs(seed: int = 0, part: int = 0) -> dict:
    keys = jax.random.split(jax.random.key(seed), 10)
    part_keys = jax.random.split(jax.random.fold_in(keys[9], part), 10)
    return {
        "centres": draw_centres(jax.random.fold_in(jax.random.fold_in(keys[9], part), 71), part),
        "factor": scatter_about(part_keys[1], (9, G), 0.008, 0.048, ((1, 16),), jnp.float32),
        "harmonics": scatter_about(part_keys[2], (HARMONICS, G), 0.6, 3.6, ((1, 16),), jnp.float32),
        "opacity": jnp.clip(-4.0 + 4.0 * jax.random.uniform(part_keys[3], (G,), jnp.float32) ** block_scale(part_keys[3], (G,), ((0, 16),), -0.2, 0.2), -4.0, 0.0),
        "cameras": draw_cameras(jax.random.fold_in(jax.random.fold_in(keys[9], part), 71), part),
        "requests": draw_requests(jax.random.fold_in(jax.random.fold_in(keys[9], part), 71), part),
        "tile_lists": draw_tile_lists(jax.random.fold_in(jax.random.fold_in(keys[9], part), 71), part),
        "tile_ids": draw_tile_ids(jax.random.fold_in(jax.random.fold_in(keys[9], part), 71), part),
        "image_cotangent": scatter_about(part_keys[8], (3, TILES, PIX), 1.0, 6.0, ((1, 16),), jnp.float32),
    }


UPPER_LIMIT = lax.Precision.HIGHEST
BAND_ONE = 0.4886025119029199

def sh_basis(dir_x, dir_y, dir_z):
    sq_x = dir_x * dir_x
    sq_y = dir_y * dir_y
    sq_z = dir_z * dir_z
    return [jnp.full_like(dir_x, 0.28209479177387814), -BAND_ONE * dir_y, BAND_ONE * dir_z, -BAND_ONE * dir_x, 1.0925484305920792 * dir_x * dir_y, -1.0925484305920792 * dir_y * dir_z, 0.31539156525252005 * (2.0 * sq_z - sq_x - sq_y), -1.0925484305920792 * dir_x * dir_z, 0.5462742152960396 * (sq_x - sq_y), -0.5900435899266435 * dir_y * (3.0 * sq_x - sq_y), 2.890611442640554 * dir_x * dir_y * dir_z, -0.4570457994644658 * dir_y * (4.0 * sq_z - sq_x - sq_y), 0.3731763325901154 * dir_z * (2.0 * sq_z - 3.0 * sq_x - 3.0 * sq_y), -0.4570457994644658 * dir_x * (4.0 * sq_z - sq_x - sq_y), 1.445305721320277 * dir_z * (sq_x - sq_y), -0.5900435899266435 * dir_x * (sq_x - 3.0 * sq_y)]

def combine(harmonic, coeffs, channel):
    summed = jnp.full_like(harmonic[0], 0.5)
    for number in range(16):
        summed = summed + harmonic[number] * coeffs[16 * channel + number]
    return summed

def preprocess(positions, shapes, coeffs, logits, cameras):
    covariance_matrix = [[shapes[3 * line_a] * shapes[3 * line_b] + shapes[3 * line_a + 1] * shapes[3 * line_b + 1] + shapes[3 * line_a + 2] * shapes[3 * line_b + 2] for line_b in range(3)] for line_a in range(3)]
    opaque = jax.nn.sigmoid(logits)
    stacked = []
    for camera in range(cameras.shape[0]):
        rel_x = positions[0] - cameras[camera, 0]
        rel_y = positions[1] - cameras[camera, 1]
        rel_z = positions[2] - cameras[camera, 2]
        inverse = 1.0 / rel_z
        screen_x = FOCAL * rel_x * inverse + 0.5 * IMG_W
        screen_y = FOCAL * rel_y * inverse + 0.5 * IMG_H
        jac_xx = FOCAL * inverse
        jac_xz = -FOCAL * rel_x * inverse * inverse
        jac_yz = -FOCAL * rel_y * inverse * inverse
        cov_a = jac_xx * jac_xx * covariance_matrix[0][0] + 2.0 * jac_xx * jac_xz * covariance_matrix[0][2] + jac_xz * jac_xz * covariance_matrix[2][2] + 0.3
        cov_b = jac_xx * jac_xx * covariance_matrix[0][1] + jac_xx * jac_yz * covariance_matrix[0][2] + jac_xz * jac_xx * covariance_matrix[2][1] + jac_xz * jac_yz * covariance_matrix[2][2]
        cov_c = jac_xx * jac_xx * covariance_matrix[1][1] + 2.0 * jac_xx * jac_yz * covariance_matrix[1][2] + jac_yz * jac_yz * covariance_matrix[2][2] + 0.3
        determ = cov_a * cov_c - cov_b * cov_b
        length = jnp.sqrt(rel_x * rel_x + rel_y * rel_y + rel_z * rel_z)
        harmonic = sh_basis(rel_x / length, rel_y / length, rel_z / length)
        colours = [combine(harmonic, coeffs, channel) for channel in range(3)]
        stacked.append(jnp.stack([screen_x, screen_y, cov_c / determ, -cov_b / determ, cov_a / determ] + colours + [opaque]))
    return jnp.stack(stacked)

def tile_pixels(tile_ids):
    per_view = TILES_ACROSS * TILE_ROWS
    remainder = tile_ids % per_view
    corner_x = remainder % TILES_ACROSS * TILE
    corner_y = remainder // TILES_ACROSS * TILE
    inside = jnp.arange(TILE * TILE, dtype=jnp.int32)
    pix_x = (corner_x[:, None] + inside[None, :] % TILE).astype(jnp.float32) + 0.5
    pix_y = (corner_y[:, None] + inside[None, :] // TILE).astype(jnp.float32) + 0.5
    return (pix_x, pix_y)

def raster(record, present, pix_x, pix_y):
    length = record.shape[2]
    strict_upper = (jnp.arange(length)[:, None] < jnp.arange(length)[None, :]).astype(jnp.float32)
    delta_x = pix_x[:, :, None] - record[:, 0][:, None, :]
    delta_y = pix_y[:, :, None] - record[:, 1][:, None, :]
    quadric = record[:, 2][:, None, :] * delta_x * delta_x + 2.0 * record[:, 3][:, None, :] * delta_x * delta_y + record[:, 4][:, None, :] * delta_y * delta_y
    falloff = jnp.exp(-0.5 * quadric)
    alphas = (record[:, 8] * present)[:, None, :] * falloff
    log_keep = jnp.log1p(-alphas)
    before = jnp.einsum('bpe,ef->bpf', log_keep, strict_upper, precision=UPPER_LIMIT)
    transmit = jnp.exp(before)
    weight = alphas * transmit
    rendered = jnp.einsum('bpe,bce->bcp', weight, record[:, 5:8], precision=UPPER_LIMIT)
    return (rendered, (falloff, alphas, transmit, weight, delta_x, delta_y, strict_upper))

def reference(centres, factor, harmonics, opacity, cameras, requests, tile_lists, tile_ids, image_cotangent):

    def project(positions, shapes, coeffs, logits):
        return preprocess(positions, shapes, coeffs, logits, cameras)
    records, pull_back = jax.vjp(project, centres, factor, harmonics, opacity)
    flat_rows = records.transpose(0, 2, 1).reshape(VIEWS * G, 9)
    holder = (jnp.arange(TILES, dtype=jnp.int32) // TILE_DEV).astype(jnp.int32)
    active = tile_lists >= 0
    lookup = jnp.where(active, tile_lists, 0).astype(jnp.int32)
    wanted = requests.reshape(N_GS, SLOTS)[holder[:, None], lookup]
    global_id = lookup // CAP * G_DEV + wanted
    view_of = tile_ids // (TILES_ACROSS * TILE_ROWS)
    flat_index = (view_of[:, None] * G + global_id).astype(jnp.int32)
    entries = flat_rows[flat_index].transpose(0, 2, 1)
    pix_x, pix_y = tile_pixels(tile_ids)
    present = active.astype(jnp.float32)

    def one_tile(pieces):
        record, mask_row, row_x, row_y, upstream = pieces

        def render(values):
            return raster(values[None], mask_row[None], row_x[None], row_y[None])[0][0]
        rendered, pull_tile = jax.vjp(render, record)
        return (rendered, pull_tile(upstream)[0])
    rendered, tile_grads = lax.map(one_tile, (entries, present, pix_x, pix_y, image_cotangent.transpose(1, 0, 2)))
    target = jnp.where(active, flat_index, VIEWS * G).reshape(-1).astype(jnp.int32)
    summed = jax.ops.segment_sum(tile_grads.transpose(0, 2, 1).reshape(-1, 9), target, num_segments=VIEWS * G)
    record_grads = summed.reshape(VIEWS, G, 9).transpose(0, 2, 1)
    grad_centres, grad_factor, grad_harmonics, grad_opacity = pull_back(record_grads)
    return (rendered.transpose(1, 0, 2), grad_centres, grad_factor, grad_harmonics, grad_opacity)
```

```python
import functools

import jax
import jax.numpy as jnp
from jax import lax
from jax.experimental import pallas as pl
from jax.experimental.pallas import tpu as pltpu
from jax.sharding import PartitionSpec as P

TILE = 16
PIX = TILE * TILE
IMG_W = 960
IMG_H = 540
FOCAL = 600
TILES_ACROSS = 60
TILE_ROWS = 33
VIEWS = 4
CAP = 32
LANES = 128
SEGS = LANES // CAP
ROWS = 16
CHUNK = 512
F32 = jnp.float32
BF16 = jnp.bfloat16
VMEM_LIMIT = 48 * 1024 * 1024

BAND_ONE = 0.4886025119029199


def sh_basis(dir_x, dir_y, dir_z):
    sq_x = dir_x * dir_x
    sq_y = dir_y * dir_y
    sq_z = dir_z * dir_z
    return [
        jnp.full_like(dir_x, 0.28209479177387814),
        -BAND_ONE * dir_y,
        BAND_ONE * dir_z,
        -BAND_ONE * dir_x,
        1.0925484305920792 * dir_x * dir_y,
        -1.0925484305920792 * dir_y * dir_z,
        0.31539156525252005 * (2.0 * sq_z - sq_x - sq_y),
        -1.0925484305920792 * dir_x * dir_z,
        0.5462742152960396 * (sq_x - sq_y),
        -0.5900435899266435 * dir_y * (3.0 * sq_x - sq_y),
        2.890611442640554 * dir_x * dir_y * dir_z,
        -0.4570457994644658 * dir_y * (4.0 * sq_z - sq_x - sq_y),
        0.3731763325901154 * dir_z * (2.0 * sq_z - 3.0 * sq_x - 3.0 * sq_y),
        -0.4570457994644658 * dir_x * (4.0 * sq_z - sq_x - sq_y),
        1.445305721320277 * dir_z * (sq_x - sq_y),
        -0.5900435899266435 * dir_x * (sq_x - 3.0 * sq_y),
    ]


def geometry(pos, shape, cam):
    cov = [
        [
            shape[3 * i] * shape[3 * j]
            + shape[3 * i + 1] * shape[3 * j + 1]
            + shape[3 * i + 2] * shape[3 * j + 2]
            for j in range(3)
        ]
        for i in range(3)
    ]
    rel_x = pos[0] - cam[0]
    rel_y = pos[1] - cam[1]
    rel_z = pos[2] - cam[2]
    inverse = 1.0 / rel_z
    screen_x = FOCAL * rel_x * inverse + 0.5 * IMG_W
    screen_y = FOCAL * rel_y * inverse + 0.5 * IMG_H
    jac_xx = FOCAL * inverse
    jac_xz = -FOCAL * rel_x * inverse * inverse
    jac_yz = -FOCAL * rel_y * inverse * inverse
    cov_a = (
        jac_xx * jac_xx * cov[0][0]
        + 2.0 * jac_xx * jac_xz * cov[0][2]
        + jac_xz * jac_xz * cov[2][2]
        + 0.3
    )
    cov_b = (
        jac_xx * jac_xx * cov[0][1]
        + jac_xx * jac_yz * cov[0][2]
        + jac_xz * jac_xx * cov[2][1]
        + jac_xz * jac_yz * cov[2][2]
    )
    cov_c = (
        jac_xx * jac_xx * cov[1][1]
        + 2.0 * jac_xx * jac_yz * cov[1][2]
        + jac_yz * jac_yz * cov[2][2]
        + 0.3
    )
    scale = 1.0 / (cov_a * cov_c - cov_b * cov_b)
    shrink = 1.0 / jnp.sqrt(rel_x * rel_x + rel_y * rel_y + rel_z * rel_z)
    basis = sh_basis(rel_x * shrink, rel_y * shrink, rel_z * shrink)
    return [screen_x, screen_y, cov_c * scale, -cov_b * scale, cov_a * scale], basis


def split(value, parts):
    out = []
    for _ in range(parts - 1):
        piece = value.astype(BF16)
        out.append(piece)
        value = value - piece.astype(F32)
    out.append(value.astype(BF16))
    return out


def mm(a, b):
    return jnp.dot(a, b, preferred_element_type=F32)


def mm_nt(a, b):
    return lax.dot_general(a, b, (((1,), (1,)), ((), ())), preferred_element_type=F32)


def mm_tn(a, b):
    return lax.dot_general(a, b, (((0,), (0,)), ((), ())), preferred_element_type=F32)


def swap_segments(arrays):
    seg = lax.broadcasted_iota(jnp.int32, arrays[0].shape, 1) // CAP
    turned = [[a if s == 0 else pltpu.roll(a, CAP * s, 1) for s in range(SEGS)] for a in arrays]
    out = []
    for o in range(SEGS):
        z = turned[0][(0 - o) % SEGS]
        for v in range(1, SEGS):
            z = jnp.where(seg == v, turned[v][(v - o) % SEGS], z)
        out.append(z)
    return out


def one_hot(base, index, rows):
    ids = lax.broadcasted_iota(jnp.int32, (rows, index.shape[1]), 0) + base
    return jnp.where(ids == index, 1.0, 0.0).astype(BF16)


def raw_rows(raw):
    def row(i):
        return raw[i : i + 1]
    return (
        [row(57 + i) for i in range(3)],
        [row(48 + i) for i in range(9)],
        [row(i) for i in range(48)],
        row(60),
    )


def camera_columns(cam_ref):
    return [cam_ref[:, i : i + 1] for i in range(3)]


def project_kernel(want_ref, cen_ref, fac_ref, har_ref, opa_ref, cam_ref, rec_ref, raw_ref, parts_ref):
    gauss = cen_ref.shape[1]
    for base in range(0, gauss, CHUNK):
        cols = slice(base, base + CHUNK)
        whole = jnp.concatenate(
            [har_ref[:, cols], fac_ref[:, cols], cen_ref[:, cols], opa_ref[:, cols],
             jnp.zeros((3, CHUNK), F32)], axis=0)
        parts_ref[:, cols] = jnp.concatenate(split(whole, 3), axis=0)
    want = jnp.maximum(want_ref[...], 0)
    acc = jnp.zeros((192, CHUNK), F32)
    for base in range(0, gauss, CHUNK):
        acc = acc + mm(parts_ref[:, base : base + CHUNK], one_hot(base, want, CHUNK))
    raw = acc[0:64] + acc[64:128] + acc[128:192]
    raw_ref[...] = raw
    pos, shape, coeffs, logit = raw_rows(raw)
    records, basis = geometry(pos, shape, camera_columns(cam_ref))
    for c in range(3):
        summed = jnp.full_like(basis[0], 0.5)
        for j in range(16):
            summed = summed + basis[j] * coeffs[16 * c + j]
        records.append(summed)
    strength = 1.0 / (1.0 + jnp.exp(-logit))
    records.append(jnp.broadcast_to(strength, (VIEWS, CHUNK)))
    blank = jnp.zeros((ROWS - 9, CHUNK), F32)
    by_view = [jnp.concatenate([r[v : v + 1] for r in records] + [blank], axis=0) for v in range(VIEWS)]
    for b in range(CHUNK // LANES):
        swapped = swap_segments([x[:, b * LANES : (b + 1) * LANES] for x in by_view])
        for o in range(SEGS):
            rec_ref[b * SEGS + o] = swapped[o]


def pull_kernel(want_ref, back_ref, raw_ref, cam_ref, cen_ref, fac_ref, har_ref, opa_ref):
    gauss = cen_ref.shape[1]
    by_view = [[] for _ in range(VIEWS)]
    for b in range(CHUNK // LANES):
        swapped = swap_segments([back_ref[b * SEGS + o] for o in range(SEGS)])
        for v in range(VIEWS):
            by_view[v].append(swapped[v])
    by_view = [jnp.concatenate(x, axis=1) for x in by_view]
    grads = [jnp.concatenate([by_view[v][c : c + 1] for v in range(VIEWS)], axis=0) for c in range(9)]
    pos, shape, coeffs, logit = raw_rows(raw_ref[...])
    cam = camera_columns(cam_ref)
    (_, basis), pull = jax.vjp(lambda p, s: geometry(p, s, cam), pos, shape)
    basis_grads = []
    for j in range(16):
        total = grads[5] * coeffs[j]
        for c in range(1, 3):
            total = total + grads[5 + c] * coeffs[16 * c + j]
        basis_grads.append(total)
    pos_grads, shape_grads = pull((grads[:5], basis_grads))
    rows = [
        jnp.sum(grads[5 + c] * basis[j], axis=0, keepdims=True) for c in range(3) for j in range(16)
    ]
    rows += list(shape_grads) + list(pos_grads)
    keep = 1.0 - 1.0 / (1.0 + jnp.exp(-logit))
    rows.append(keep * jnp.sum(grads[8], axis=0, keepdims=True))
    rows.append(jnp.zeros((3, CHUNK), F32))
    parts = jnp.concatenate(split(jnp.concatenate(rows, axis=0), 2), axis=0)
    want = want_ref[...]
    first = pl.program_id(0) == 0
    for base in range(0, gauss, CHUNK):
        cols = slice(base, base + CHUNK)
        both = mm_nt(parts, one_hot(base, want, CHUNK))
        total = both[0:64] + both[64:128]

        def put(ref, value):
            @pl.when(first)
            def _():
                ref[:, cols] = value

            @pl.when(jnp.logical_not(first))
            def _():
                ref[:, cols] = ref[:, cols] + value

        put(har_ref, total[0:48])
        put(fac_ref, total[48:57])
        put(cen_ref, total[57:60])
        put(opa_ref, total[60:61])


def loop(count, body):
    if count == 1:
        body(0)
    else:
        def step(i, carry):
            body(i)
            return carry
        lax.fori_loop(0, count, step, 0)


def aligned(i, size):
    return i * size if isinstance(i, int) else pl.multiple_of(i * size, size)


def raster_kernel(
    ids_ref, rec_ref, list_ref, cot_ref, img_ref, back_ref,
    rec_s, sel_s, grad_s, lk_s, alpha_s, ratio_s, shade_s, before_s, w_s, sw_s, swp_s,
):
    owners = rec_ref.shape[0]
    slots = owners * CAP
    tiles, length = list_ref.shape
    half = length // 2

    def unpack(b):
        swapped = swap_segments([rec_ref[b * SEGS + o] for o in range(SEGS)])
        for v in range(VIEWS):
            rec_s[v, :, pl.ds(aligned(b, LANES), LANES)] = jnp.concatenate(split(swapped[v], 3), axis=0)

    if owners <= 16:
        for b in range(owners // SEGS):
            unpack(b)
    else:
        loop(owners // SEGS, unpack)
    grad_s[...] = jnp.zeros_like(grad_s)

    row_i = lax.broadcasted_iota(jnp.int32, (length, length), 0)
    col_i = lax.broadcasted_iota(jnp.int32, (length, length), 1)
    upper = jnp.where(row_i < col_i, 1.0, 0.0).astype(BF16)
    lower = jnp.where(row_i > col_i, 1.0, 0.0).astype(BF16)
    px = lax.broadcasted_iota(jnp.int32, (TILE, length), 0).astype(F32) + 0.5

    def tile(t):
        code = ids_ref[t]
        view = code // (TILES_ACROSS * TILE_ROWS)
        place = code - view * (TILES_ACROSS * TILE_ROWS)
        line = place // TILES_ACROSS
        corner_y = (line * TILE).astype(F32)
        corner_x = ((place - line * TILES_ACROSS) * TILE).astype(F32)
        entries = list_ref[pl.ds(t, 1), :]
        got = [jnp.zeros((3 * ROWS, length), F32)]

        def gather(c):
            at = pl.ds(aligned(c, CHUNK), CHUNK)
            sel = one_hot(c * CHUNK, entries, CHUNK)
            sel_s[at, :] = sel
            return mm(rec_s[view, :, at], sel)

        if slots == CHUNK:
            got = gather(0)
        else:
            got = lax.fori_loop(
                0, slots // CHUNK, lambda c, a: a + gather(c), jnp.zeros((3 * ROWS, length), F32))
        rec = got[0:ROWS] + got[ROWS : 2 * ROWS] + got[2 * ROWS :]
        con_a, con_b, con_c = rec[2:3], rec[3:4], rec[4:5]
        colour = rec[5:8]
        strength = rec[8:9]
        dx = (corner_x + px) - rec[0:1]
        dy = (corner_y + px) - rec[1:2]
        quad_x = (-0.5 * con_a) * dx * dx
        cross = (-con_b) * dx
        quad_y = (-0.5 * con_c) * dy * dy
        for y in range(TILE):
            rows = slice(y * TILE, (y + 1) * TILE)
            falloff = jnp.exp(quad_x + cross * dy[y : y + 1] + quad_y[y : y + 1])
            alpha = strength * falloff
            keep = jnp.log(1.0 - alpha)
            alpha_s[rows] = alpha
            ratio_s[rows] = alpha * jnp.exp(-keep)
            hi, lo = split(keep, 2)
            lk_s[0, rows] = hi
            lk_s[1, rows] = lo
        before_s[:, :half] = mm(lk_s[0, :, :half], upper[:half, :half]) + mm(
            lk_s[1, :, :half], upper[:half, :half])
        before_s[:, half:] = mm(lk_s[0], upper[:, half:]) + mm(lk_s[1], upper[:, half:])

        cot = jnp.concatenate([cot_ref[c, pl.ds(t, 1), :] for c in range(3)], axis=0)
        cot_hi, cot_lo = split(cot, 2)
        col_hi, col_lo = split(colour, 2)
        pad = jnp.zeros((ROWS - 9, PIX), BF16)
        shade_s[...] = mm_tn(
            jnp.concatenate([cot_hi, cot_hi, cot_lo, pad], axis=0),
            jnp.concatenate([col_hi, col_lo, col_hi, jnp.zeros((ROWS - 9, length), BF16)], axis=0),
        )
        for y in range(TILE):
            rows = slice(y * TILE, (y + 1) * TILE)
            weight = alpha_s[rows] * jnp.exp(before_s[rows])
            hi, lo = split(weight, 2)
            w_s[0, rows] = hi
            w_s[1, rows] = lo
            shaded = shade_s[rows] * weight
            sw_s[rows] = shaded
            hi, lo = split(shaded, 2)
            swp_s[0, rows] = hi
            swp_s[1, rows] = lo
        before_s[:, half:] = mm(swp_s[0, :, half:], lower[half:, half:]) + mm(
            swp_s[1, :, half:], lower[half:, half:])
        before_s[:, :half] = mm(swp_s[0], lower[:, :half]) + mm(swp_s[1], lower[:, :half])

        six = jnp.zeros((2, length), BF16)
        col_parts = jnp.concatenate([col_hi, col_lo, six], axis=0)
        by_hi = mm_nt(col_parts, w_s[0])
        by_lo = mm_nt(col_parts, w_s[1])
        image = by_hi[0:3] + by_hi[3:6] + by_lo[0:3]
        for c in range(3):
            img_ref[c, pl.ds(t, 1), :] = image[c : c + 1]
        cot_parts = jnp.concatenate([cot_hi, cot_lo, jnp.zeros((2, PIX), BF16)], axis=0)
        by_hi = mm(cot_parts, w_s[0])
        by_lo = mm(cot_parts, w_s[1])
        grad_colour = by_hi[0:3] + by_hi[3:6] + by_lo[0:3]

        sum_0 = jnp.zeros((TILE, length), F32)
        sum_1 = jnp.zeros((TILE, length), F32)
        sum_2 = jnp.zeros((TILE, length), F32)
        for y in range(TILE):
            rows = slice(y * TILE, (y + 1) * TILE)
            g = sw_s[rows] - before_s[rows] * ratio_s[rows]
            g_y = g * dy[y : y + 1]
            sum_0 = sum_0 + g
            sum_1 = sum_1 + g_y
            sum_2 = sum_2 + g_y * dy[y : y + 1]

        def total(value):
            return jnp.sum(value, axis=0, keepdims=True)

        m_x = sum_0 * dx
        m_0, m_10, m_20 = total(sum_0), total(m_x), total(m_x * dx)
        m_01, m_11, m_02 = total(sum_1), total(sum_1 * dx), total(sum_2)
        back = jnp.concatenate(
            [
                con_a * m_10 + con_b * m_01,
                con_b * m_10 + con_c * m_01,
                -0.5 * m_20,
                -m_11,
                -0.5 * m_02,
                grad_colour,
                m_0,
                jnp.zeros((ROWS - 9, length), F32),
            ],
            axis=0,
        )
        parts = jnp.concatenate(split(back, 2), axis=0)

        def scatter(c):
            at = pl.ds(aligned(c, CHUNK), CHUNK)
            both = mm_nt(parts, sel_s[at, :])
            grad_s[view, :, at] = grad_s[view, :, at] + both[0:ROWS] + both[ROWS:]

        loop(slots // CHUNK, scatter)

    loop(tiles, tile)

    def pack(b):
        swapped = swap_segments([grad_s[v, :, pl.ds(aligned(b, LANES), LANES)] for v in range(VIEWS)])
        for o in range(SEGS):
            back_ref[b * SEGS + o] = swapped[o]

    if owners <= 16:
        for b in range(owners // SEGS):
            pack(b)
    else:
        loop(owners // SEGS, pack)


def whole(shape):
    return pl.BlockSpec(shape, lambda i: (0,) * len(shape))


def local(
    centres, factor, harmonics, opacity, cameras, requests, tile_lists, tile_ids, image_cotangent
):
    gauss = centres.shape[1]
    slots = requests.shape[0]
    owners = slots // CAP
    tiles, length = tile_lists.shape
    chunks = slots // CHUNK
    params = pltpu.CompilerParams(vmem_limit_bytes=VMEM_LIMIT)
    wanted = lax.all_to_all(requests, "gs", split_axis=0, concat_axis=0, tiled=True).reshape(1, slots)

    want_spec = pl.BlockSpec((1, CHUNK), lambda i: (0, i))
    block_spec = pl.BlockSpec((CHUNK // CAP, ROWS, LANES), lambda i: (i, 0, 0))
    raw_spec = pl.BlockSpec((64, CHUNK), lambda i: (0, i))
    owned = [whole((3, gauss)), whole((9, gauss)), whole((48, gauss)), whole((1, gauss))]
    block_type = jax.ShapeDtypeStruct((owners, ROWS, LANES), F32)

    picked, raw = pl.pallas_call(
        project_kernel,
        grid=(chunks,),
        in_specs=[want_spec] + owned + [whole((VIEWS, 3))],
        out_specs=[block_spec, raw_spec],
        out_shape=[block_type, jax.ShapeDtypeStruct((64, slots), F32)],
        scratch_shapes=[pltpu.VMEM((192, gauss), BF16)],
        compiler_params=params,
    )(wanted, centres, factor, harmonics, opacity.reshape(1, gauss), cameras)
    records = lax.all_to_all(picked, "gs", split_axis=0, concat_axis=0, tiled=True)

    vmem = pl.BlockSpec(memory_space=pltpu.VMEM)
    image, back = pl.pallas_call(
        raster_kernel,
        in_specs=[pl.BlockSpec(memory_space=pltpu.SMEM), vmem, vmem, vmem],
        out_specs=[vmem, vmem],
        out_shape=[jax.ShapeDtypeStruct((3, tiles, PIX), F32), block_type],
        scratch_shapes=[
            pltpu.VMEM((VIEWS, 3 * ROWS, slots), BF16),
            pltpu.VMEM((slots, length), BF16),
            pltpu.VMEM((VIEWS, ROWS, slots), F32),
            pltpu.VMEM((2, PIX, length), BF16),
            pltpu.VMEM((PIX, length), F32),
            pltpu.VMEM((PIX, length), F32),
            pltpu.VMEM((PIX, length), F32),
            pltpu.VMEM((PIX, length), F32),
            pltpu.VMEM((2, PIX, length), BF16),
            pltpu.VMEM((PIX, length), F32),
            pltpu.VMEM((2, PIX, length), BF16),
        ],
        compiler_params=params,
    )(tile_ids, records, tile_lists, image_cotangent)
    returned = lax.all_to_all(back, "gs", split_axis=0, concat_axis=0, tiled=True)

    grads = pl.pallas_call(
        pull_kernel,
        grid=(chunks,),
        in_specs=[want_spec, block_spec, raw_spec, whole((VIEWS, 3))],
        out_specs=owned,
        out_shape=[jax.ShapeDtypeStruct((n, gauss), F32) for n in (3, 9, 48, 1)],
        compiler_params=params,
    )(wanted, returned, raw, cameras)
    return (image, grads[0], grads[1], grads[2], grads[3].reshape(gauss))


def solution(mesh):
    in_specs = (
        P(None, ("grp", "gs")),
        P(None, ("grp", "gs")),
        P(None, ("grp", "gs")),
        P(("grp", "gs")),
        P("grp", None),
        P(("grp", "gs")),
        P(("grp", "gs"), None),
        P(("grp", "gs")),
        P(None, ("grp", "gs"), None),
    )
    out_specs = (
        P(None, ("grp", "gs"), None),
        P(None, ("grp", "gs")),
        P(None, ("grp", "gs")),
        P(None, ("grp", "gs")),
        P(("grp", "gs")),
    )
    return jax.shard_map(local, mesh=mesh, in_specs=in_specs, out_specs=out_specs, check_vma=False)
```

```python
import functools

import jax
import jax.numpy as jnp
from jax import lax
from jax.experimental import pallas as pl
from jax.experimental.pallas import tpu as pltpu
from jax.sharding import PartitionSpec as P

TILE = 16
PIX = TILE * TILE
IMG_W = 960
IMG_H = 540
FOCAL = 600
TILES_ACROSS = 60
TILE_ROWS = 33
VIEWS = 4
CAP = 32
LANES = 128
SEGS = LANES // CAP
ROWS = 16
CHUNK = 512
F32 = jnp.float32
BF16 = jnp.bfloat16
VMEM_LIMIT = 48 * 1024 * 1024

BAND_ONE = 0.4886025119029199


def sh_basis(dir_x, dir_y, dir_z):
    sq_x = dir_x * dir_x
    sq_y = dir_y * dir_y
    sq_z = dir_z * dir_z
    return [
        jnp.full_like(dir_x, 0.28209479177387814),
        -BAND_ONE * dir_y,
        BAND_ONE * dir_z,
        -BAND_ONE * dir_x,
        1.0925484305920792 * dir_x * dir_y,
        -1.0925484305920792 * dir_y * dir_z,
        0.31539156525252005 * (2.0 * sq_z - sq_x - sq_y),
        -1.0925484305920792 * dir_x * dir_z,
        0.5462742152960396 * (sq_x - sq_y),
        -0.5900435899266435 * dir_y * (3.0 * sq_x - sq_y),
        2.890611442640554 * dir_x * dir_y * dir_z,
        -0.4570457994644658 * dir_y * (4.0 * sq_z - sq_x - sq_y),
        0.3731763325901154 * dir_z * (2.0 * sq_z - 3.0 * sq_x - 3.0 * sq_y),
        -0.4570457994644658 * dir_x * (4.0 * sq_z - sq_x - sq_y),
        1.445305721320277 * dir_z * (sq_x - sq_y),
        -0.5900435899266435 * dir_x * (sq_x - 3.0 * sq_y),
    ]


def geometry(pos, shape, cam):
    cov = [
        [
            shape[3 * i] * shape[3 * j]
            + shape[3 * i + 1] * shape[3 * j + 1]
            + shape[3 * i + 2] * shape[3 * j + 2]
            for j in range(3)
        ]
        for i in range(3)
    ]
    rel_x = pos[0] - cam[0]
    rel_y = pos[1] - cam[1]
    rel_z = pos[2] - cam[2]
    inverse = 1.0 / rel_z
    screen_x = FOCAL * rel_x * inverse + 0.5 * IMG_W
    screen_y = FOCAL * rel_y * inverse + 0.5 * IMG_H
    jac_xx = FOCAL * inverse
    jac_xz = -FOCAL * rel_x * inverse * inverse
    jac_yz = -FOCAL * rel_y * inverse * inverse
    cov_a = (
        jac_xx * jac_xx * cov[0][0]
        + 2.0 * jac_xx * jac_xz * cov[0][2]
        + jac_xz * jac_xz * cov[2][2]
        + 0.3
    )
    cov_b = (
        jac_xx * jac_xx * cov[0][1]
        + jac_xx * jac_yz * cov[0][2]
        + jac_xz * jac_xx * cov[2][1]
        + jac_xz * jac_yz * cov[2][2]
    )
    cov_c = (
        jac_xx * jac_xx * cov[1][1]
        + 2.0 * jac_xx * jac_yz * cov[1][2]
        + jac_yz * jac_yz * cov[2][2]
        + 0.3
    )
    scale = 1.0 / (cov_a * cov_c - cov_b * cov_b)
    shrink = 1.0 / jnp.sqrt(rel_x * rel_x + rel_y * rel_y + rel_z * rel_z)
    basis = sh_basis(rel_x * shrink, rel_y * shrink, rel_z * shrink)
    return [screen_x, screen_y, cov_c * scale, -cov_b * scale, cov_a * scale], basis


def split(value, parts):
    out = []
    for _ in range(parts - 1):
        piece = value.astype(BF16)
        out.append(piece)
        value = value - piece.astype(F32)
    out.append(value.astype(BF16))
    return out


def mm(a, b):
    return jnp.dot(a, b, preferred_element_type=F32)


def mm_nt(a, b):
    return lax.dot_general(a, b, (((1,), (1,)), ((), ())), preferred_element_type=F32)


def mm_tn(a, b):
    return lax.dot_general(a, b, (((0,), (0,)), ((), ())), preferred_element_type=F32)


def swap_segments(arrays):
    seg = lax.broadcasted_iota(jnp.int32, arrays[0].shape, 1) // CAP
    turned = [[a if s == 0 else pltpu.roll(a, CAP * s, 1) for s in range(SEGS)] for a in arrays]
    out = []
    for o in range(SEGS):
        z = turned[0][(0 - o) % SEGS]
        for v in range(1, SEGS):
            z = jnp.where(seg == v, turned[v][(v - o) % SEGS], z)
        out.append(z)
    return out


def one_hot(base, index, rows):
    ids = lax.broadcasted_iota(jnp.int32, (rows, index.shape[1]), 0) + base
    return jnp.where(ids == index, 1.0, 0.0).astype(BF16)


def raw_rows(raw):
    def row(i):
        return raw[i : i + 1]
    return (
        [row(57 + i) for i in range(3)],
        [row(48 + i) for i in range(9)],
        [row(i) for i in range(48)],
        row(60),
    )


def camera_columns(cam_ref):
    return [cam_ref[:, i : i + 1] for i in range(3)]


def partners(owners, body):
    me = lax.axis_index("gs")

    def step(i, carry):
        body(lax.rem(me + i, owners))
        return carry

    lax.fori_loop(1, owners, step, 0, unroll=owners <= 16)


def greet(owners):
    barrier = pltpu.get_barrier_semaphore()
    partners(owners, lambda p: pl.semaphore_signal(
        barrier, inc=1, device_id={"gs": p}, device_id_type=pl.DeviceIdType.MESH))
    return barrier


def block_copy(source, target, send_sem, recv_sem, sender, partner):
    return pltpu.make_async_remote_copy(
        src_ref=source, dst_ref=target, send_sem=send_sem.at[partner], recv_sem=recv_sem.at[sender],
        device_id={"gs": partner}, device_id_type=pl.DeviceIdType.MESH)


def swap_blocks(owners, source, target, send_sem, recv_sem):
    me = lax.axis_index("gs")
    partners(owners, lambda p: block_copy(
        source(p), target.at[me], send_sem, recv_sem, me, p).start())

    def finish():
        partners(owners, lambda p: block_copy(
            source(p), target.at[p], send_sem, recv_sem, p, p).wait_recv())
        partners(owners, lambda p: block_copy(
            source(p), target.at[me], send_sem, recv_sem, me, p).wait_send())

    return finish


def project_kernel(
    req_ref, cen_hbm, fac_hbm, har_hbm, opa_hbm, cam_ref, rec_ref, raw_ref, want_ref,
    cen_ref, fac_ref, har_ref, opa_ref, parts_ref, got_ref, ask_ref, out_ref,
    load_sem, ask_send, ask_recv, rec_send, rec_recv,
):
    owners = rec_ref.shape[0]
    gauss = cen_ref.shape[1]
    me = lax.axis_index("gs")
    loads = [
        pltpu.make_async_copy(src, dst, load_sem.at[i])
        for i, (src, dst) in enumerate(
            [(cen_hbm, cen_ref), (fac_hbm, fac_ref), (har_hbm, har_ref), (opa_hbm, opa_ref)])
    ]
    for load in loads:
        load.start()
    barrier = greet(owners)
    pl.semaphore_wait(barrier, owners - 1)
    finish = swap_blocks(owners, lambda p: req_ref.at[p // SEGS], got_ref, ask_send, ask_recv)
    got_ref[me] = req_ref[me // SEGS]
    for load in loads:
        load.wait()
    for base in range(0, gauss, CHUNK):
        cols = slice(base, base + CHUNK)
        whole = jnp.concatenate(
            [har_ref[:, cols], fac_ref[:, cols], cen_ref[:, cols], opa_ref[:, cols],
             jnp.zeros((3, CHUNK), F32)], axis=0)
        parts_ref[:, cols] = jnp.concatenate(split(whole, 3), axis=0)
    finish()
    seg = lax.broadcasted_iota(jnp.int32, (owners, LANES), 1) // CAP
    row = lax.broadcasted_iota(jnp.int32, (owners, LANES), 0)
    mine = jnp.where(seg == lax.rem(me, SEGS), got_ref[:, 0, :], 0)
    spread = mine
    for s in range(1, SEGS):
        spread = spread + pltpu.roll(mine, CAP * s, 1)
    ask_ref[...] = jnp.where(seg == lax.rem(row, SEGS), spread, 0)

    def project(c):
        near = ask_ref[pl.ds(aligned(c, CHUNK // CAP), CHUNK // CAP), :]
        asked = jnp.concatenate(
            [jnp.sum(near[b * SEGS : (b + 1) * SEGS], axis=0, keepdims=True)
             for b in range(CHUNK // LANES)], axis=1)
        lanes = pl.ds(aligned(c, CHUNK), CHUNK)
        want_ref[:, lanes] = asked
        want = jnp.maximum(asked, 0)
        acc = jnp.zeros((192, CHUNK), F32)
        for base in range(0, gauss, CHUNK):
            acc = acc + mm(parts_ref[:, base : base + CHUNK], one_hot(base, want, CHUNK))
        raw = acc[0:64] + acc[64:128] + acc[128:192]
        raw_ref[:, lanes] = raw
        pos, shape, coeffs, logit = raw_rows(raw)
        records, basis = geometry(pos, shape, camera_columns(cam_ref))
        for ch in range(3):
            summed = jnp.full_like(basis[0], 0.5)
            for j in range(16):
                summed = summed + basis[j] * coeffs[16 * ch + j]
            records.append(summed)
        strength = 1.0 / (1.0 + jnp.exp(-logit))
        records.append(jnp.broadcast_to(strength, (VIEWS, CHUNK)))
        blank = jnp.zeros((ROWS - 9, CHUNK), F32)
        by_view = [
            jnp.concatenate([r[v : v + 1] for r in records] + [blank], axis=0) for v in range(VIEWS)]
        for b in range(CHUNK // LANES):
            swapped = swap_segments([x[:, b * LANES : (b + 1) * LANES] for x in by_view])
            for o in range(SEGS):
                out_ref[c * (CHUNK // CAP) + b * SEGS + o] = swapped[o]

    loop(owners * CAP // CHUNK, project)
    finish = swap_blocks(owners, lambda p: out_ref.at[p], rec_ref, rec_send, rec_recv)
    rec_ref[me] = out_ref[me]
    finish()


def swap_kernel(in_ref, out_ref, send_sem, recv_sem):
    owners = in_ref.shape[0]
    me = lax.axis_index("gs")
    barrier = greet(owners)
    pl.semaphore_wait(barrier, owners - 1)
    finish = swap_blocks(owners, lambda p: in_ref.at[p], out_ref, send_sem, recv_sem)
    out_ref[me] = in_ref[me]
    finish()


def pull_kernel(want_ref, back_ref, raw_ref, cam_ref, cen_ref, fac_ref, har_ref, opa_ref):
    gauss = cen_ref.shape[1]
    by_view = [[] for _ in range(VIEWS)]
    for b in range(CHUNK // LANES):
        swapped = swap_segments([back_ref[b * SEGS + o] for o in range(SEGS)])
        for v in range(VIEWS):
            by_view[v].append(swapped[v])
    by_view = [jnp.concatenate(x, axis=1) for x in by_view]
    grads = [jnp.concatenate([by_view[v][c : c + 1] for v in range(VIEWS)], axis=0) for c in range(9)]
    pos, shape, coeffs, logit = raw_rows(raw_ref[...])
    cam = camera_columns(cam_ref)
    (_, basis), pull = jax.vjp(lambda p, s: geometry(p, s, cam), pos, shape)
    basis_grads = []
    for j in range(16):
        total = grads[5] * coeffs[j]
        for c in range(1, 3):
            total = total + grads[5 + c] * coeffs[16 * c + j]
        basis_grads.append(total)
    pos_grads, shape_grads = pull((grads[:5], basis_grads))
    rows = [
        jnp.sum(grads[5 + c] * basis[j], axis=0, keepdims=True) for c in range(3) for j in range(16)
    ]
    rows += list(shape_grads) + list(pos_grads)
    keep = 1.0 - 1.0 / (1.0 + jnp.exp(-logit))
    rows.append(keep * jnp.sum(grads[8], axis=0, keepdims=True))
    rows.append(jnp.zeros((3, CHUNK), F32))
    parts = jnp.concatenate(split(jnp.concatenate(rows, axis=0), 2), axis=0)
    want = want_ref[...]
    first = pl.program_id(0) == 0
    for base in range(0, gauss, CHUNK):
        cols = slice(base, base + CHUNK)
        both = mm_nt(parts, one_hot(base, want, CHUNK))
        total = both[0:64] + both[64:128]

        def put(ref, value):
            @pl.when(first)
            def _():
                ref[:, cols] = value

            @pl.when(jnp.logical_not(first))
            def _():
                ref[:, cols] = ref[:, cols] + value

        put(har_ref, total[0:48])
        put(fac_ref, total[48:57])
        put(cen_ref, total[57:60])
        put(opa_ref, total[60:61])


def loop(count, body):
    if count == 1:
        body(0)
    else:
        def step(i, carry):
            body(i)
            return carry
        lax.fori_loop(0, count, step, 0)


def aligned(i, size):
    return i * size if isinstance(i, int) else pl.multiple_of(i * size, size)


def raster_kernel(
    ids_ref, rec_ref, list_ref, cot_ref, img_ref, back_ref,
    rec_s, sel_s, grad_s, lk_s, alpha_s, ratio_s, shade_s, before_s, w_s, sw_s, swp_s,
):
    owners = rec_ref.shape[0]
    slots = owners * CAP
    tiles, length = list_ref.shape
    half = length // 2

    def unpack(b):
        swapped = swap_segments([rec_ref[b * SEGS + o] for o in range(SEGS)])
        for v in range(VIEWS):
            rec_s[v, :, pl.ds(aligned(b, LANES), LANES)] = jnp.concatenate(split(swapped[v], 3), axis=0)

    if owners <= 16:
        for b in range(owners // SEGS):
            unpack(b)
    else:
        loop(owners // SEGS, unpack)
    grad_s[...] = jnp.zeros_like(grad_s)

    row_i = lax.broadcasted_iota(jnp.int32, (length, length), 0)
    col_i = lax.broadcasted_iota(jnp.int32, (length, length), 1)
    upper = jnp.where(row_i < col_i, 1.0, 0.0).astype(BF16)
    lower = jnp.where(row_i > col_i, 1.0, 0.0).astype(BF16)
    px = lax.broadcasted_iota(jnp.int32, (TILE, length), 0).astype(F32) + 0.5

    def tile(t):
        code = ids_ref[t]
        view = code // (TILES_ACROSS * TILE_ROWS)
        place = code - view * (TILES_ACROSS * TILE_ROWS)
        line = place // TILES_ACROSS
        corner_y = (line * TILE).astype(F32)
        corner_x = ((place - line * TILES_ACROSS) * TILE).astype(F32)
        entries = list_ref[pl.ds(t, 1), :]
        got = [jnp.zeros((3 * ROWS, length), F32)]

        def gather(c):
            at = pl.ds(aligned(c, CHUNK), CHUNK)
            sel = one_hot(c * CHUNK, entries, CHUNK)
            sel_s[at, :] = sel
            return mm(rec_s[view, :, at], sel)

        if slots == CHUNK:
            got = gather(0)
        else:
            got = lax.fori_loop(
                0, slots // CHUNK, lambda c, a: a + gather(c), jnp.zeros((3 * ROWS, length), F32))
        rec = got[0:ROWS] + got[ROWS : 2 * ROWS] + got[2 * ROWS :]
        con_a, con_b, con_c = rec[2:3], rec[3:4], rec[4:5]
        colour = rec[5:8]
        strength = rec[8:9]
        dx = (corner_x + px) - rec[0:1]
        dy = (corner_y + px) - rec[1:2]
        quad_x = (-0.5 * con_a) * dx * dx
        cross = (-con_b) * dx
        quad_y = (-0.5 * con_c) * dy * dy
        for y in range(TILE):
            rows = slice(y * TILE, (y + 1) * TILE)
            falloff = jnp.exp(quad_x + cross * dy[y : y + 1] + quad_y[y : y + 1])
            alpha = strength * falloff
            keep = jnp.log(1.0 - alpha)
            alpha_s[rows] = alpha
            ratio_s[rows] = alpha * jnp.exp(-keep)
            hi, lo = split(keep, 2)
            lk_s[0, rows] = hi
            lk_s[1, rows] = lo
        before_s[:, :half] = mm(lk_s[0, :, :half], upper[:half, :half]) + mm(
            lk_s[1, :, :half], upper[:half, :half])
        before_s[:, half:] = mm(lk_s[0], upper[:, half:]) + mm(lk_s[1], upper[:, half:])

        cot = jnp.concatenate([cot_ref[c, pl.ds(t, 1), :] for c in range(3)], axis=0)
        cot_hi, cot_lo = split(cot, 2)
        col_hi, col_lo = split(colour, 2)
        pad = jnp.zeros((ROWS - 9, PIX), BF16)
        shade_s[...] = mm_tn(
            jnp.concatenate([cot_hi, cot_hi, cot_lo, pad], axis=0),
            jnp.concatenate([col_hi, col_lo, col_hi, jnp.zeros((ROWS - 9, length), BF16)], axis=0),
        )
        for y in range(TILE):
            rows = slice(y * TILE, (y + 1) * TILE)
            weight = alpha_s[rows] * jnp.exp(before_s[rows])
            hi, lo = split(weight, 2)
            w_s[0, rows] = hi
            w_s[1, rows] = lo
            shaded = shade_s[rows] * weight
            sw_s[rows] = shaded
            hi, lo = split(shaded, 2)
            swp_s[0, rows] = hi
            swp_s[1, rows] = lo
        before_s[:, half:] = mm(swp_s[0, :, half:], lower[half:, half:]) + mm(
            swp_s[1, :, half:], lower[half:, half:])
        before_s[:, :half] = mm(swp_s[0], lower[:, :half]) + mm(swp_s[1], lower[:, :half])

        six = jnp.zeros((2, length), BF16)
        col_parts = jnp.concatenate([col_hi, col_lo, six], axis=0)
        by_hi = mm_nt(col_parts, w_s[0])
        by_lo = mm_nt(col_parts, w_s[1])
        image = by_hi[0:3] + by_hi[3:6] + by_lo[0:3]
        for c in range(3):
            img_ref[c, pl.ds(t, 1), :] = image[c : c + 1]
        cot_parts = jnp.concatenate([cot_hi, cot_lo, jnp.zeros((2, PIX), BF16)], axis=0)
        by_hi = mm(cot_parts, w_s[0])
        by_lo = mm(cot_parts, w_s[1])
        grad_colour = by_hi[0:3] + by_hi[3:6] + by_lo[0:3]

        sum_0 = jnp.zeros((TILE, length), F32)
        sum_1 = jnp.zeros((TILE, length), F32)
        sum_2 = jnp.zeros((TILE, length), F32)
        for y in range(TILE):
            rows = slice(y * TILE, (y + 1) * TILE)
            g = sw_s[rows] - before_s[rows] * ratio_s[rows]
            g_y = g * dy[y : y + 1]
            sum_0 = sum_0 + g
            sum_1 = sum_1 + g_y
            sum_2 = sum_2 + g_y * dy[y : y + 1]

        def total(value):
            return jnp.sum(value, axis=0, keepdims=True)

        m_x = sum_0 * dx
        m_0, m_10, m_20 = total(sum_0), total(m_x), total(m_x * dx)
        m_01, m_11, m_02 = total(sum_1), total(sum_1 * dx), total(sum_2)
        back = jnp.concatenate(
            [
                con_a * m_10 + con_b * m_01,
                con_b * m_10 + con_c * m_01,
                -0.5 * m_20,
                -m_11,
                -0.5 * m_02,
                grad_colour,
                m_0,
                jnp.zeros((ROWS - 9, length), F32),
            ],
            axis=0,
        )
        parts = jnp.concatenate(split(back, 2), axis=0)

        def scatter(c):
            at = pl.ds(aligned(c, CHUNK), CHUNK)
            both = mm_nt(parts, sel_s[at, :])
            grad_s[view, :, at] = grad_s[view, :, at] + both[0:ROWS] + both[ROWS:]

        loop(slots // CHUNK, scatter)

    loop(tiles, tile)

    def pack(b):
        swapped = swap_segments([grad_s[v, :, pl.ds(aligned(b, LANES), LANES)] for v in range(VIEWS)])
        for o in range(SEGS):
            back_ref[b * SEGS + o] = swapped[o]

    if owners <= 16:
        for b in range(owners // SEGS):
            pack(b)
    else:
        loop(owners // SEGS, pack)


def whole(shape):
    return pl.BlockSpec(shape, lambda i: (0,) * len(shape))


def local(
    centres, factor, harmonics, opacity, cameras, requests, tile_lists, tile_ids, image_cotangent
):
    gauss = centres.shape[1]
    slots = requests.shape[0]
    owners = slots // CAP
    tiles, length = tile_lists.shape
    chunks = slots // CHUNK
    params = pltpu.CompilerParams(vmem_limit_bytes=VMEM_LIMIT)
    want_spec = pl.BlockSpec((1, CHUNK), lambda i: (0, i))
    block_spec = pl.BlockSpec((CHUNK // CAP, ROWS, LANES), lambda i: (i, 0, 0))
    raw_spec = pl.BlockSpec((64, CHUNK), lambda i: (0, i))
    owned = [whole((3, gauss)), whole((9, gauss)), whole((48, gauss)), whole((1, gauss))]
    block_type = jax.ShapeDtypeStruct((owners, ROWS, LANES), F32)

    vmem = pl.BlockSpec(memory_space=pltpu.VMEM)
    hbm = pl.BlockSpec(memory_space=pltpu.HBM)
    sems = pltpu.SemaphoreType.DMA((owners,))
    records, raw, wanted = pl.pallas_call(
        project_kernel,
        in_specs=[vmem, hbm, hbm, hbm, hbm, vmem],
        out_specs=[vmem, vmem, vmem],
        out_shape=[
            block_type,
            jax.ShapeDtypeStruct((64, slots), F32),
            jax.ShapeDtypeStruct((1, slots), jnp.int32),
        ],
        scratch_shapes=[
            pltpu.VMEM((3, gauss), F32),
            pltpu.VMEM((9, gauss), F32),
            pltpu.VMEM((48, gauss), F32),
            pltpu.VMEM((1, gauss), F32),
            pltpu.VMEM((192, gauss), BF16),
            pltpu.VMEM((owners, 1, LANES), jnp.int32),
            pltpu.VMEM((owners, LANES), jnp.int32),
            pltpu.VMEM((owners, ROWS, LANES), F32),
            pltpu.SemaphoreType.DMA((4,)),
            sems, sems, sems, sems,
        ],
        compiler_params=pltpu.CompilerParams(
            vmem_limit_bytes=VMEM_LIMIT, collective_id=0, has_side_effects=True),
    )(
        requests.reshape(slots // LANES, 1, LANES), centres, factor, harmonics,
        opacity.reshape(1, gauss), cameras,
    )

    image, back = pl.pallas_call(
        raster_kernel,
        in_specs=[pl.BlockSpec(memory_space=pltpu.SMEM), vmem, vmem, vmem],
        out_specs=[vmem, vmem],
        out_shape=[jax.ShapeDtypeStruct((3, tiles, PIX), F32), block_type],
        scratch_shapes=[
            pltpu.VMEM((VIEWS, 3 * ROWS, slots), BF16),
            pltpu.VMEM((slots, length), BF16),
            pltpu.VMEM((VIEWS, ROWS, slots), F32),
            pltpu.VMEM((2, PIX, length), BF16),
            pltpu.VMEM((PIX, length), F32),
            pltpu.VMEM((PIX, length), F32),
            pltpu.VMEM((PIX, length), F32),
            pltpu.VMEM((PIX, length), F32),
            pltpu.VMEM((2, PIX, length), BF16),
            pltpu.VMEM((PIX, length), F32),
            pltpu.VMEM((2, PIX, length), BF16),
        ],
        compiler_params=params,
    )(tile_ids, records, tile_lists, image_cotangent)
    returned = pl.pallas_call(
        swap_kernel,
        in_specs=[vmem],
        out_specs=vmem,
        out_shape=block_type,
        scratch_shapes=[sems, sems],
        compiler_params=pltpu.CompilerParams(collective_id=1, has_side_effects=True),
    )(back)

    grads = pl.pallas_call(
        pull_kernel,
        grid=(chunks,),
        in_specs=[want_spec, block_spec, raw_spec, whole((VIEWS, 3))],
        out_specs=owned,
        out_shape=[jax.ShapeDtypeStruct((n, gauss), F32) for n in (3, 9, 48, 1)],
        compiler_params=params,
    )(wanted, returned, raw, cameras)
    return (image, grads[0], grads[1], grads[2], grads[3].reshape(gauss))


def solution(mesh):
    in_specs = (
        P(None, ("grp", "gs")),
        P(None, ("grp", "gs")),
        P(None, ("grp", "gs")),
        P(("grp", "gs")),
        P("grp", None),
        P(("grp", "gs")),
        P(("grp", "gs"), None),
        P(("grp", "gs")),
        P(None, ("grp", "gs"), None),
    )
    out_specs = (
        P(None, ("grp", "gs"), None),
        P(None, ("grp", "gs")),
        P(None, ("grp", "gs")),
        P(None, ("grp", "gs")),
        P(("grp", "gs")),
    )
    return jax.shard_map(local, mesh=mesh, in_specs=in_specs, out_specs=out_specs, check_vma=False)
```

```python
import functools

import jax
import jax.numpy as jnp
from jax import lax
from jax.experimental import pallas as pl
from jax.experimental.pallas import tpu as pltpu
from jax.sharding import PartitionSpec as P

TILE = 16
PIX = TILE * TILE
IMG_W = 960
IMG_H = 540
FOCAL = 600
TILES_ACROSS = 60
TILE_ROWS = 33
VIEWS = 4
CAP = 32
LANES = 128
SEGS = LANES // CAP
ROWS = 16
CHUNK = 512
F32 = jnp.float32
BF16 = jnp.bfloat16
VMEM_LIMIT = 60 * 1024 * 1024
FIELDS = 9

BAND_ONE = 0.4886025119029199


def sh_basis(dir_x, dir_y, dir_z):
    sq_x = dir_x * dir_x
    sq_y = dir_y * dir_y
    sq_z = dir_z * dir_z
    return [
        jnp.full_like(dir_x, 0.28209479177387814),
        -BAND_ONE * dir_y,
        BAND_ONE * dir_z,
        -BAND_ONE * dir_x,
        1.0925484305920792 * dir_x * dir_y,
        -1.0925484305920792 * dir_y * dir_z,
        0.31539156525252005 * (2.0 * sq_z - sq_x - sq_y),
        -1.0925484305920792 * dir_x * dir_z,
        0.5462742152960396 * (sq_x - sq_y),
        -0.5900435899266435 * dir_y * (3.0 * sq_x - sq_y),
        2.890611442640554 * dir_x * dir_y * dir_z,
        -0.4570457994644658 * dir_y * (4.0 * sq_z - sq_x - sq_y),
        0.3731763325901154 * dir_z * (2.0 * sq_z - 3.0 * sq_x - 3.0 * sq_y),
        -0.4570457994644658 * dir_x * (4.0 * sq_z - sq_x - sq_y),
        1.445305721320277 * dir_z * (sq_x - sq_y),
        -0.5900435899266435 * dir_x * (sq_x - 3.0 * sq_y),
    ]


def geometry(pos, shape, cam):
    cov = [
        [
            shape[3 * i] * shape[3 * j]
            + shape[3 * i + 1] * shape[3 * j + 1]
            + shape[3 * i + 2] * shape[3 * j + 2]
            for j in range(3)
        ]
        for i in range(3)
    ]
    rel_x = pos[0] - cam[0]
    rel_y = pos[1] - cam[1]
    rel_z = pos[2] - cam[2]
    inverse = 1.0 / rel_z
    screen_x = FOCAL * rel_x * inverse + 0.5 * IMG_W
    screen_y = FOCAL * rel_y * inverse + 0.5 * IMG_H
    jac_xx = FOCAL * inverse
    jac_xz = -FOCAL * rel_x * inverse * inverse
    jac_yz = -FOCAL * rel_y * inverse * inverse
    cov_a = (
        jac_xx * jac_xx * cov[0][0]
        + 2.0 * jac_xx * jac_xz * cov[0][2]
        + jac_xz * jac_xz * cov[2][2]
        + 0.3
    )
    cov_b = (
        jac_xx * jac_xx * cov[0][1]
        + jac_xx * jac_yz * cov[0][2]
        + jac_xz * jac_xx * cov[2][1]
        + jac_xz * jac_yz * cov[2][2]
    )
    cov_c = (
        jac_xx * jac_xx * cov[1][1]
        + 2.0 * jac_xx * jac_yz * cov[1][2]
        + jac_yz * jac_yz * cov[2][2]
        + 0.3
    )
    scale = 1.0 / (cov_a * cov_c - cov_b * cov_b)
    shrink = 1.0 / jnp.sqrt(rel_x * rel_x + rel_y * rel_y + rel_z * rel_z)
    basis = sh_basis(rel_x * shrink, rel_y * shrink, rel_z * shrink)
    return [screen_x, screen_y, cov_c * scale, -cov_b * scale, cov_a * scale], basis


def split(value, parts):
    out = []
    for _ in range(parts - 1):
        piece = value.astype(BF16)
        out.append(piece)
        value = value - piece.astype(F32)
    out.append(value.astype(BF16))
    return out


def mm(a, b):
    return jnp.dot(a, b, preferred_element_type=F32)


def mm_nt(a, b):
    return lax.dot_general(a, b, (((1,), (1,)), ((), ())), preferred_element_type=F32)


def mm_tn(a, b):
    return lax.dot_general(a, b, (((0,), (0,)), ((), ())), preferred_element_type=F32)


def swap_segments(arrays):
    seg = lax.broadcasted_iota(jnp.int32, arrays[0].shape, 1) // CAP
    turned = [[a if s == 0 else pltpu.roll(a, CAP * s, 1) for s in range(SEGS)] for a in arrays]
    out = []
    for o in range(SEGS):
        z = turned[0][(0 - o) % SEGS]
        for v in range(1, SEGS):
            z = jnp.where(seg == v, turned[v][(v - o) % SEGS], z)
        out.append(z)
    return out


def one_hot(base, index, rows):
    ids = lax.broadcasted_iota(jnp.int32, (rows, index.shape[1]), 0) + base
    return jnp.where(ids == index, 1.0, 0.0).astype(BF16)


def raw_rows(raw):
    def row(i):
        return raw[i : i + 1]
    return (
        [row(57 + i) for i in range(3)],
        [row(48 + i) for i in range(9)],
        [row(i) for i in range(48)],
        row(60),
    )


def camera_columns(cam_ref):
    return [cam_ref[:, i : i + 1] for i in range(3)]


def partners(owners, body):
    me = lax.axis_index("gs")

    def step(i, carry):
        body(lax.rem(me + i, owners))
        return carry

    lax.fori_loop(1, owners, step, 0, unroll=owners <= 16)


def greet(owners):
    barrier = pltpu.get_barrier_semaphore()
    partners(owners, lambda p: pl.semaphore_signal(
        barrier, inc=1, device_id={"gs": p}, device_id_type=pl.DeviceIdType.MESH))
    return barrier


def block_copy(source, target, send_sem, recv_sem, sender, partner):
    return pltpu.make_async_remote_copy(
        src_ref=source, dst_ref=target, send_sem=send_sem.at[partner], recv_sem=recv_sem.at[sender],
        device_id={"gs": partner}, device_id_type=pl.DeviceIdType.MESH)


def swap_blocks(owners, source, target, send_sem, recv_sem):
    me = lax.axis_index("gs")
    partners(owners, lambda p: block_copy(
        source(p), target.at[me], send_sem, recv_sem, me, p).start())

    def finish():
        partners(owners, lambda p: block_copy(
            source(p), target.at[p], send_sem, recv_sem, p, p).wait_recv())
        partners(owners, lambda p: block_copy(
            source(p), target.at[me], send_sem, recv_sem, me, p).wait_send())

    return finish


def splat_kernel(
    req_hbm, cen_hbm, fac_hbm, har_hbm, opa_hbm, cam_hbm, ids_hbm, list_hbm, cot_hbm,
    img_ref, back_ref, raw_ref, want_ref,
    req_ref, cen_ref, fac_ref, har_ref, opa_ref, cam_ref, ids_ref, list_ref, cot_ref,
    parts_ref, got_ref, ask_ref, out_ref, rec_ref,
    rec_s, sel_s, grad_s, lk_s, alpha_s, ratio_s, shade_s, before_s, w_s, sw_s, swp_s,
    load_sem, ask_send, ask_recv, rec_send, rec_recv, back_send, back_recv,
):
    owners = rec_ref.shape[0]
    gauss = cen_ref.shape[1]
    me = lax.axis_index("gs")
    loads = [
        pltpu.make_async_copy(src, dst, load_sem.at[i])
        for i, (src, dst) in enumerate([
            (req_hbm, req_ref), (har_hbm, har_ref), (fac_hbm, fac_ref), (cen_hbm, cen_ref),
            (opa_hbm, opa_ref), (cam_hbm, cam_ref), (ids_hbm, ids_ref), (list_hbm, list_ref),
            (cot_hbm, cot_ref)])
    ]
    for load in loads:
        load.start()
    barrier = greet(owners)
    loads[0].wait()
    pl.semaphore_wait(barrier, owners - 1)
    finish = swap_blocks(owners, lambda p: req_ref.at[p // SEGS], got_ref, ask_send, ask_recv)
    got_ref[me] = req_ref[me // SEGS]
    for load in loads[1:]:
        load.wait()
    for base in range(0, gauss, CHUNK):
        cols = slice(base, base + CHUNK)
        whole = jnp.concatenate(
            [har_ref[:, cols], fac_ref[:, cols], cen_ref[:, cols], opa_ref[:, cols],
             jnp.zeros((3, CHUNK), F32)], axis=0)
        parts_ref[:, cols] = jnp.concatenate(split(whole, 3), axis=0)
    finish()
    seg = lax.broadcasted_iota(jnp.int32, (owners, LANES), 1) // CAP
    row = lax.broadcasted_iota(jnp.int32, (owners, LANES), 0)
    mine = jnp.where(seg == lax.rem(me, SEGS), got_ref[:, 0, :], 0)
    spread = mine
    for s in range(1, SEGS):
        spread = spread + pltpu.roll(mine, CAP * s, 1)
    ask_ref[...] = jnp.where(seg == lax.rem(row, SEGS), spread, 0)

    def project(c):
        near = ask_ref[pl.ds(aligned(c, CHUNK // CAP), CHUNK // CAP), :]
        asked = jnp.concatenate(
            [jnp.sum(near[b * SEGS : (b + 1) * SEGS], axis=0, keepdims=True)
             for b in range(CHUNK // LANES)], axis=1)
        lanes = pl.ds(aligned(c, CHUNK), CHUNK)
        want_ref[:, lanes] = asked
        want = jnp.maximum(asked, 0)
        acc = jnp.zeros((192, CHUNK), F32)
        for base in range(0, gauss, CHUNK):
            acc = acc + mm(parts_ref[:, base : base + CHUNK], one_hot(base, want, CHUNK))
        raw = acc[0:64] + acc[64:128] + acc[128:192]
        raw_ref[:, lanes] = raw
        pos, shape, coeffs, logit = raw_rows(raw)
        records, basis = geometry(pos, shape, camera_columns(cam_ref))
        for ch in range(3):
            summed = jnp.full_like(basis[0], 0.5)
            for j in range(16):
                summed = summed + basis[j] * coeffs[16 * ch + j]
            records.append(summed)
        strength = 1.0 / (1.0 + jnp.exp(-logit))
        records.append(jnp.broadcast_to(strength, (VIEWS, CHUNK)))
        blank = jnp.zeros((ROWS - 9, CHUNK), F32)
        by_view = [
            jnp.concatenate([r[v : v + 1] for r in records] + [blank], axis=0) for v in range(VIEWS)]
        for b in range(CHUNK // LANES):
            swapped = swap_segments([x[:, b * LANES : (b + 1) * LANES] for x in by_view])
            for o in range(SEGS):
                out_ref[c * (CHUNK // CAP) + b * SEGS + o] = swapped[o][0:FIELDS]

    loop(owners * CAP // CHUNK, project)
    finish = swap_blocks(owners, lambda p: out_ref.at[p], rec_ref, rec_send, rec_recv)
    rec_ref[me] = out_ref[me]
    finish()
    raster(
        ids_ref, rec_ref, list_ref, cot_ref, img_ref, out_ref,
        rec_s, sel_s, grad_s, lk_s, alpha_s, ratio_s, shade_s, before_s, w_s, sw_s, swp_s,
    )
    finish = swap_blocks(owners, lambda p: out_ref.at[p], back_ref, back_send, back_recv)
    back_ref[me] = out_ref[me]
    finish()


def pull_kernel(want_ref, back_ref, raw_ref, cam_ref, img_ref, cen_ref, fac_ref, har_ref, opa_ref, out_ref):
    gauss = cen_ref.shape[1]
    out_ref[...] = img_ref[...]
    by_view = [[] for _ in range(VIEWS)]
    for b in range(CHUNK // LANES):
        swapped = swap_segments([back_ref[b * SEGS + o] for o in range(SEGS)])
        for v in range(VIEWS):
            by_view[v].append(swapped[v])
    by_view = [jnp.concatenate(x, axis=1) for x in by_view]
    grads = [jnp.concatenate([by_view[v][c : c + 1] for v in range(VIEWS)], axis=0) for c in range(9)]
    pos, shape, coeffs, logit = raw_rows(raw_ref[...])
    cam = camera_columns(cam_ref)
    (_, basis), pull = jax.vjp(lambda p, s: geometry(p, s, cam), pos, shape)
    basis_grads = []
    for j in range(16):
        total = grads[5] * coeffs[j]
        for c in range(1, 3):
            total = total + grads[5 + c] * coeffs[16 * c + j]
        basis_grads.append(total)
    pos_grads, shape_grads = pull((grads[:5], basis_grads))
    rows = [
        jnp.sum(grads[5 + c] * basis[j], axis=0, keepdims=True) for c in range(3) for j in range(16)
    ]
    rows += list(shape_grads) + list(pos_grads)
    keep = 1.0 - 1.0 / (1.0 + jnp.exp(-logit))
    rows.append(keep * jnp.sum(grads[8], axis=0, keepdims=True))
    rows.append(jnp.zeros((3, CHUNK), F32))
    parts = jnp.concatenate(split(jnp.concatenate(rows, axis=0), 2), axis=0)
    want = want_ref[...]
    first = pl.program_id(0) == 0
    for base in range(0, gauss, CHUNK):
        cols = slice(base, base + CHUNK)
        both = mm_nt(parts, one_hot(base, want, CHUNK))
        total = both[0:64] + both[64:128]

        def put(ref, value):
            @pl.when(first)
            def _():
                ref[:, cols] = value

            @pl.when(jnp.logical_not(first))
            def _():
                ref[:, cols] = ref[:, cols] + value

        put(har_ref, total[0:48])
        put(fac_ref, total[48:57])
        put(cen_ref, total[57:60])
        put(opa_ref, total[60:61])


def loop(count, body):
    if count == 1:
        body(0)
    else:
        def step(i, carry):
            body(i)
            return carry
        lax.fori_loop(0, count, step, 0)


def aligned(i, size):
    return i * size if isinstance(i, int) else pl.multiple_of(i * size, size)


def raster(
    ids_ref, rec_ref, list_ref, cot_ref, img_ref, back_ref,
    rec_s, sel_s, grad_s, lk_s, alpha_s, ratio_s, shade_s, before_s, w_s, sw_s, swp_s,
):
    owners = rec_ref.shape[0]
    slots = owners * CAP
    tiles, length = list_ref.shape
    half = length // 2
    blank = jnp.zeros((ROWS - FIELDS, LANES), F32)

    def unpack(b):
        swapped = swap_segments([rec_ref[b * SEGS + o] for o in range(SEGS)])
        for v in range(VIEWS):
            rec_s[v, :, pl.ds(aligned(b, LANES), LANES)] = jnp.concatenate(
                split(jnp.concatenate([swapped[v], blank], axis=0), 3), axis=0)

    if owners <= 16:
        for b in range(owners // SEGS):
            unpack(b)
    else:
        loop(owners // SEGS, unpack)
    grad_s[...] = jnp.zeros_like(grad_s)

    row_i = lax.broadcasted_iota(jnp.int32, (length, length), 0)
    col_i = lax.broadcasted_iota(jnp.int32, (length, length), 1)
    upper = jnp.where(row_i < col_i, 1.0, 0.0).astype(BF16)
    lower = jnp.where(row_i > col_i, 1.0, 0.0).astype(BF16)
    px = lax.broadcasted_iota(jnp.int32, (TILE, length), 0).astype(F32) + 0.5

    def tile(t):
        code = ids_ref[t]
        view = code // (TILES_ACROSS * TILE_ROWS)
        place = code - view * (TILES_ACROSS * TILE_ROWS)
        line = place // TILES_ACROSS
        corner_y = (line * TILE).astype(F32)
        corner_x = ((place - line * TILES_ACROSS) * TILE).astype(F32)
        entries = list_ref[pl.ds(t, 1), :]
        got = [jnp.zeros((3 * ROWS, length), F32)]

        def gather(c):
            at = pl.ds(aligned(c, CHUNK), CHUNK)
            sel = one_hot(c * CHUNK, entries, CHUNK)
            sel_s[at, :] = sel
            return mm(rec_s[view, :, at], sel)

        if slots == CHUNK:
            got = gather(0)
        else:
            got = lax.fori_loop(
                0, slots // CHUNK, lambda c, a: a + gather(c), jnp.zeros((3 * ROWS, length), F32))
        rec = got[0:ROWS] + got[ROWS : 2 * ROWS] + got[2 * ROWS :]
        con_a, con_b, con_c = rec[2:3], rec[3:4], rec[4:5]
        colour = rec[5:8]
        strength = rec[8:9]
        dx = (corner_x + px) - rec[0:1]
        dy = (corner_y + px) - rec[1:2]
        quad_x = (-0.5 * con_a) * dx * dx
        cross = (-con_b) * dx
        quad_y = (-0.5 * con_c) * dy * dy
        for y in range(TILE):
            rows = slice(y * TILE, (y + 1) * TILE)
            falloff = jnp.exp(quad_x + cross * dy[y : y + 1] + quad_y[y : y + 1])
            alpha = strength * falloff
            keep = jnp.log(1.0 - alpha)
            alpha_s[rows] = alpha
            ratio_s[rows] = alpha * jnp.exp(-keep)
            hi, lo = split(keep, 2)
            lk_s[0, rows] = hi
            lk_s[1, rows] = lo
        before_s[:, :half] = mm(lk_s[0, :, :half], upper[:half, :half]) + mm(
            lk_s[1, :, :half], upper[:half, :half])
        before_s[:, half:] = mm(lk_s[0], upper[:, half:]) + mm(lk_s[1], upper[:, half:])

        cot = jnp.concatenate([cot_ref[c, pl.ds(t, 1), :] for c in range(3)], axis=0)
        cot_hi, cot_lo = split(cot, 2)
        col_hi, col_lo = split(colour, 2)
        pad = jnp.zeros((ROWS - 9, PIX), BF16)
        shade_s[...] = mm_tn(
            jnp.concatenate([cot_hi, cot_hi, cot_lo, pad], axis=0),
            jnp.concatenate([col_hi, col_lo, col_hi, jnp.zeros((ROWS - 9, length), BF16)], axis=0),
        )
        for y in range(TILE):
            rows = slice(y * TILE, (y + 1) * TILE)
            weight = alpha_s[rows] * jnp.exp(before_s[rows])
            hi, lo = split(weight, 2)
            w_s[0, rows] = hi
            w_s[1, rows] = lo
            shaded = shade_s[rows] * weight
            sw_s[rows] = shaded
            hi, lo = split(shaded, 2)
            swp_s[0, rows] = hi
            swp_s[1, rows] = lo
        before_s[:, half:] = mm(swp_s[0, :, half:], lower[half:, half:]) + mm(
            swp_s[1, :, half:], lower[half:, half:])
        before_s[:, :half] = mm(swp_s[0], lower[:, :half]) + mm(swp_s[1], lower[:, :half])

        six = jnp.zeros((2, length), BF16)
        col_parts = jnp.concatenate([col_hi, col_lo, six], axis=0)
        by_hi = mm_nt(col_parts, w_s[0])
        by_lo = mm_nt(col_parts, w_s[1])
        image = by_hi[0:3] + by_hi[3:6] + by_lo[0:3]
        for c in range(3):
            img_ref[c, pl.ds(t, 1), :] = image[c : c + 1]
        cot_parts = jnp.concatenate([cot_hi, cot_lo, jnp.zeros((2, PIX), BF16)], axis=0)
        by_hi = mm(cot_parts, w_s[0])
        by_lo = mm(cot_parts, w_s[1])
        grad_colour = by_hi[0:3] + by_hi[3:6] + by_lo[0:3]

        sum_0 = jnp.zeros((TILE, length), F32)
        sum_1 = jnp.zeros((TILE, length), F32)
        sum_2 = jnp.zeros((TILE, length), F32)
        for y in range(TILE):
            rows = slice(y * TILE, (y + 1) * TILE)
            g = sw_s[rows] - before_s[rows] * ratio_s[rows]
            g_y = g * dy[y : y + 1]
            sum_0 = sum_0 + g
            sum_1 = sum_1 + g_y
            sum_2 = sum_2 + g_y * dy[y : y + 1]

        def total(value):
            return jnp.sum(value, axis=0, keepdims=True)

        m_x = sum_0 * dx
        m_0, m_10, m_20 = total(sum_0), total(m_x), total(m_x * dx)
        m_01, m_11, m_02 = total(sum_1), total(sum_1 * dx), total(sum_2)
        back = jnp.concatenate(
            [
                con_a * m_10 + con_b * m_01,
                con_b * m_10 + con_c * m_01,
                -0.5 * m_20,
                -m_11,
                -0.5 * m_02,
                grad_colour,
                m_0,
                jnp.zeros((ROWS - 9, length), F32),
            ],
            axis=0,
        )
        parts = jnp.concatenate(split(back, 2), axis=0)

        def scatter(c):
            at = pl.ds(aligned(c, CHUNK), CHUNK)
            both = mm_nt(parts, sel_s[at, :])
            added = both[0:ROWS] + both[ROWS:]
            for v in range(VIEWS):
                grad_s[v, :, at] = grad_s[v, :, at] + jnp.where(view == v, added, 0.0)

        loop(slots // CHUNK, scatter)

    loop(tiles, tile)

    def pack(b):
        swapped = swap_segments([grad_s[v, :, pl.ds(aligned(b, LANES), LANES)] for v in range(VIEWS)])
        for o in range(SEGS):
            back_ref[b * SEGS + o] = swapped[o][0:FIELDS]

    if owners <= 16:
        for b in range(owners // SEGS):
            pack(b)
    else:
        loop(owners // SEGS, pack)


def whole(shape):
    return pl.BlockSpec(shape, lambda i: (0,) * len(shape))


def local(
    centres, factor, harmonics, opacity, cameras, requests, tile_lists, tile_ids, image_cotangent
):
    gauss = centres.shape[1]
    slots = requests.shape[0]
    owners = slots // CAP
    tiles, length = tile_lists.shape
    chunks = slots // CHUNK
    params = pltpu.CompilerParams(vmem_limit_bytes=VMEM_LIMIT)
    want_spec = pl.BlockSpec((1, CHUNK), lambda i: (0, i))
    block_spec = pl.BlockSpec((CHUNK // CAP, FIELDS, LANES), lambda i: (i, 0, 0))
    raw_spec = pl.BlockSpec((64, CHUNK), lambda i: (0, i))
    owned = [whole((3, gauss)), whole((9, gauss)), whole((48, gauss)), whole((1, gauss))]
    block_type = jax.ShapeDtypeStruct((owners, FIELDS, LANES), F32)

    vmem = pl.BlockSpec(memory_space=pltpu.VMEM)
    sems = pltpu.SemaphoreType.DMA((owners,))
    blocks = pltpu.VMEM((owners, FIELDS, LANES), F32)
    plane = pltpu.VMEM((PIX, length), F32)
    pair = pltpu.VMEM((2, PIX, length), BF16)
    image_type = jax.ShapeDtypeStruct((3, tiles, PIX), F32)
    image, returned, raw, wanted = pl.pallas_call(
        splat_kernel,
        in_specs=[pl.BlockSpec(memory_space=pl.ANY)] * 9,
        out_specs=[vmem] * 4,
        out_shape=[
            image_type,
            block_type,
            jax.ShapeDtypeStruct((64, slots), F32),
            jax.ShapeDtypeStruct((1, slots), jnp.int32),
        ],
        scratch_shapes=[
            pltpu.VMEM((slots // LANES, 1, LANES), jnp.int32),
            pltpu.VMEM((3, gauss), F32),
            pltpu.VMEM((9, gauss), F32),
            pltpu.VMEM((48, gauss), F32),
            pltpu.VMEM((1, gauss), F32),
            pltpu.VMEM((VIEWS, 3), F32),
            pltpu.SMEM((tiles,), jnp.int32),
            pltpu.VMEM((tiles, length), jnp.int32),
            pltpu.VMEM((3, tiles, PIX), F32),
            pltpu.VMEM((192, gauss), BF16),
            pltpu.VMEM((owners, 1, LANES), jnp.int32),
            pltpu.VMEM((owners, LANES), jnp.int32),
            blocks,
            blocks,
            pltpu.VMEM((VIEWS, 3 * ROWS, slots), BF16),
            pltpu.VMEM((slots, length), BF16),
            pltpu.VMEM((VIEWS, ROWS, slots), F32),
            pair, plane, plane, plane, plane, pair, plane, pair,
            pltpu.SemaphoreType.DMA((9,)),
            sems, sems, sems, sems, sems, sems,
        ],
        compiler_params=pltpu.CompilerParams(
            vmem_limit_bytes=VMEM_LIMIT, collective_id=0, has_side_effects=True),
    )(
        requests.reshape(slots // LANES, 1, LANES), centres, factor, harmonics,
        opacity.reshape(1, gauss), cameras, tile_ids, tile_lists, image_cotangent,
    )

    grads = pl.pallas_call(
        pull_kernel,
        grid=(chunks,),
        in_specs=[want_spec, block_spec, raw_spec, whole((VIEWS, 3)), whole((3, tiles, PIX))],
        out_specs=owned + [whole((3, tiles, PIX))],
        out_shape=[jax.ShapeDtypeStruct((n, gauss), F32) for n in (3, 9, 48, 1)] + [image_type],
        compiler_params=params,
    )(wanted, returned, raw, cameras, image)
    return (grads[4], grads[0], grads[1], grads[2], grads[3].reshape(gauss))


def solution(mesh):
    in_specs = (
        P(None, ("grp", "gs")),
        P(None, ("grp", "gs")),
        P(None, ("grp", "gs")),
        P(("grp", "gs")),
        P("grp", None),
        P(("grp", "gs")),
        P(("grp", "gs"), None),
        P(("grp", "gs")),
        P(None, ("grp", "gs"), None),
    )
    out_specs = (
        P(None, ("grp", "gs"), None),
        P(None, ("grp", "gs")),
        P(None, ("grp", "gs")),
        P(None, ("grp", "gs")),
        P(("grp", "gs")),
    )
    return jax.shard_map(local, mesh=mesh, in_specs=in_specs, out_specs=out_specs, check_vma=False)
```

```python
import functools

import jax
import jax.numpy as jnp
from jax import lax
from jax.experimental import pallas as pl
from jax.experimental.pallas import tpu as pltpu
from jax.sharding import PartitionSpec as P

TILE = 16
PIX = TILE * TILE
IMG_W = 960
IMG_H = 540
FOCAL = 600
TILES_ACROSS = 60
TILE_ROWS = 33
VIEWS = 4
CAP = 32
LANES = 128
SEGS = LANES // CAP
ROWS = 16
CHUNK = 512
F32 = jnp.float32
BF16 = jnp.bfloat16
VMEM_LIMIT = 60 * 1024 * 1024
FIELDS = 9
PAIR = 2
LOG2E = 1.4426950408889634

BAND_ONE = 0.4886025119029199


def sh_basis(dir_x, dir_y, dir_z):
    sq_x = dir_x * dir_x
    sq_y = dir_y * dir_y
    sq_z = dir_z * dir_z
    return [
        jnp.full_like(dir_x, 0.28209479177387814),
        -BAND_ONE * dir_y,
        BAND_ONE * dir_z,
        -BAND_ONE * dir_x,
        1.0925484305920792 * dir_x * dir_y,
        -1.0925484305920792 * dir_y * dir_z,
        0.31539156525252005 * (2.0 * sq_z - sq_x - sq_y),
        -1.0925484305920792 * dir_x * dir_z,
        0.5462742152960396 * (sq_x - sq_y),
        -0.5900435899266435 * dir_y * (3.0 * sq_x - sq_y),
        2.890611442640554 * dir_x * dir_y * dir_z,
        -0.4570457994644658 * dir_y * (4.0 * sq_z - sq_x - sq_y),
        0.3731763325901154 * dir_z * (2.0 * sq_z - 3.0 * sq_x - 3.0 * sq_y),
        -0.4570457994644658 * dir_x * (4.0 * sq_z - sq_x - sq_y),
        1.445305721320277 * dir_z * (sq_x - sq_y),
        -0.5900435899266435 * dir_x * (sq_x - 3.0 * sq_y),
    ]


def geometry(pos, shape, cam):
    cov = [
        [
            shape[3 * i] * shape[3 * j]
            + shape[3 * i + 1] * shape[3 * j + 1]
            + shape[3 * i + 2] * shape[3 * j + 2]
            for j in range(3)
        ]
        for i in range(3)
    ]
    rel_x = pos[0] - cam[0]
    rel_y = pos[1] - cam[1]
    rel_z = pos[2] - cam[2]
    inverse = 1.0 / rel_z
    screen_x = FOCAL * rel_x * inverse + 0.5 * IMG_W
    screen_y = FOCAL * rel_y * inverse + 0.5 * IMG_H
    jac_xx = FOCAL * inverse
    jac_xz = -FOCAL * rel_x * inverse * inverse
    jac_yz = -FOCAL * rel_y * inverse * inverse
    cov_a = (
        jac_xx * jac_xx * cov[0][0]
        + 2.0 * jac_xx * jac_xz * cov[0][2]
        + jac_xz * jac_xz * cov[2][2]
        + 0.3
    )
    cov_b = (
        jac_xx * jac_xx * cov[0][1]
        + jac_xx * jac_yz * cov[0][2]
        + jac_xz * jac_xx * cov[2][1]
        + jac_xz * jac_yz * cov[2][2]
    )
    cov_c = (
        jac_xx * jac_xx * cov[1][1]
        + 2.0 * jac_xx * jac_yz * cov[1][2]
        + jac_yz * jac_yz * cov[2][2]
        + 0.3
    )
    scale = 1.0 / (cov_a * cov_c - cov_b * cov_b)
    shrink = 1.0 / jnp.sqrt(rel_x * rel_x + rel_y * rel_y + rel_z * rel_z)
    basis = sh_basis(rel_x * shrink, rel_y * shrink, rel_z * shrink)
    return [screen_x, screen_y, cov_c * scale, -cov_b * scale, cov_a * scale], basis


def split(value, parts):
    out = []
    for _ in range(parts - 1):
        piece = value.astype(BF16)
        out.append(piece)
        value = value - piece.astype(F32)
    out.append(value.astype(BF16))
    return out


def mm(a, b):
    return jnp.dot(a, b, preferred_element_type=F32)


def mm_nt(a, b):
    return lax.dot_general(a, b, (((1,), (1,)), ((), ())), preferred_element_type=F32)


def mm_tn(a, b):
    return lax.dot_general(a, b, (((0,), (0,)), ((), ())), preferred_element_type=F32)


def swap_segments(arrays):
    seg = lax.broadcasted_iota(jnp.int32, arrays[0].shape, 1) // CAP
    turned = [[a if s == 0 else pltpu.roll(a, CAP * s, 1) for s in range(SEGS)] for a in arrays]
    out = []
    for o in range(SEGS):
        z = turned[0][(0 - o) % SEGS]
        for v in range(1, SEGS):
            z = jnp.where(seg == v, turned[v][(v - o) % SEGS], z)
        out.append(z)
    return out


def one_hot(base, index, rows):
    ids = lax.broadcasted_iota(jnp.int32, (rows, index.shape[1]), 0) + base
    return jnp.where(ids == index, 1.0, 0.0).astype(BF16)


def raw_rows(raw):
    def row(i):
        return raw[i : i + 1]
    return (
        [row(57 + i) for i in range(3)],
        [row(48 + i) for i in range(9)],
        [row(i) for i in range(48)],
        row(60),
    )


def camera_columns(cam_ref):
    return [cam_ref[:, i : i + 1] for i in range(3)]


def partners(owners, body):
    me = lax.axis_index("gs")

    def step(i, carry):
        body(lax.rem(me + i, owners))
        return carry

    lax.fori_loop(1, owners, step, 0, unroll=owners <= 16)


def greet(owners):
    barrier = pltpu.get_barrier_semaphore()
    partners(owners, lambda p: pl.semaphore_signal(
        barrier, inc=1, device_id={"gs": p}, device_id_type=pl.DeviceIdType.MESH))
    return barrier


def block_copy(source, target, send_sem, recv_sem, sender, partner):
    return pltpu.make_async_remote_copy(
        src_ref=source, dst_ref=target, send_sem=send_sem.at[partner], recv_sem=recv_sem.at[sender],
        device_id={"gs": partner}, device_id_type=pl.DeviceIdType.MESH)


def swap_blocks(owners, source, target, send_sem, recv_sem):
    me = lax.axis_index("gs")
    partners(owners, lambda p: block_copy(
        source(p), target.at[me], send_sem, recv_sem, me, p).start())

    def finish():
        partners(owners, lambda p: block_copy(
            source(p), target.at[p], send_sem, recv_sem, p, p).wait_recv())
        partners(owners, lambda p: block_copy(
            source(p), target.at[me], send_sem, recv_sem, me, p).wait_send())

    return finish


def splat_kernel(
    req_hbm, cen_hbm, fac_hbm, har_hbm, opa_hbm, cam_hbm, ids_hbm, list_hbm, cot_hbm,
    img_ref, back_ref, raw_ref, want_ref,
    req_ref, cen_ref, fac_ref, har_ref, opa_ref, cam_ref, ids_ref, list_ref, cot_ref,
    parts_ref, got_ref, ask_ref, out_ref, rec_ref,
    rec_s, sel_s, grad_s, lk_s, alpha_s, ratio_s, shade_s, before_s, w_s, sw_s, swp_s,
    load_sem, ask_send, ask_recv, rec_send, rec_recv, back_send, back_recv,
):
    owners = rec_ref.shape[0]
    gauss = cen_ref.shape[1]
    me = lax.axis_index("gs")
    loads = [
        pltpu.make_async_copy(src, dst, load_sem.at[i])
        for i, (src, dst) in enumerate([
            (req_hbm, req_ref), (har_hbm, har_ref), (fac_hbm, fac_ref), (cen_hbm, cen_ref),
            (opa_hbm, opa_ref), (cam_hbm, cam_ref), (ids_hbm, ids_ref), (list_hbm, list_ref),
            (cot_hbm, cot_ref)])
    ]
    for load in loads:
        load.start()
    barrier = greet(owners)
    loads[0].wait()
    pl.semaphore_wait(barrier, owners - 1)
    finish = swap_blocks(owners, lambda p: req_ref.at[p // SEGS], got_ref, ask_send, ask_recv)
    got_ref[me] = req_ref[me // SEGS]
    for load in loads[1:]:
        load.wait()
    for base in range(0, gauss, CHUNK):
        cols = slice(base, base + CHUNK)
        whole = jnp.concatenate(
            [har_ref[:, cols], fac_ref[:, cols], cen_ref[:, cols], opa_ref[:, cols],
             jnp.zeros((3, CHUNK), F32)], axis=0)
        parts_ref[:, cols] = jnp.concatenate(split(whole, 3), axis=0)
    finish()
    seg = lax.broadcasted_iota(jnp.int32, (owners, LANES), 1) // CAP
    row = lax.broadcasted_iota(jnp.int32, (owners, LANES), 0)
    mine = jnp.where(seg == lax.rem(me, SEGS), got_ref[:, 0, :], 0)
    spread = mine
    for s in range(1, SEGS):
        spread = spread + pltpu.roll(mine, CAP * s, 1)
    ask_ref[...] = jnp.where(seg == lax.rem(row, SEGS), spread, 0)

    def project(c):
        near = ask_ref[pl.ds(aligned(c, CHUNK // CAP), CHUNK // CAP), :]
        asked = jnp.concatenate(
            [jnp.sum(near[b * SEGS : (b + 1) * SEGS], axis=0, keepdims=True)
             for b in range(CHUNK // LANES)], axis=1)
        lanes = pl.ds(aligned(c, CHUNK), CHUNK)
        want_ref[:, lanes] = asked
        want = jnp.maximum(asked, 0)
        acc = jnp.zeros((192, CHUNK), F32)
        for base in range(0, gauss, CHUNK):
            acc = acc + mm(parts_ref[:, base : base + CHUNK], one_hot(base, want, CHUNK))
        raw = acc[0:64] + acc[64:128] + acc[128:192]
        raw_ref[:, lanes] = raw
        pos, shape, coeffs, logit = raw_rows(raw)
        records, basis = geometry(pos, shape, camera_columns(cam_ref))
        for ch in range(3):
            summed = jnp.full_like(basis[0], 0.5)
            for j in range(16):
                summed = summed + basis[j] * coeffs[16 * ch + j]
            records.append(summed)
        strength = 1.0 / (1.0 + jnp.exp(-logit))
        records.append(jnp.broadcast_to(strength, (VIEWS, CHUNK)))
        blank = jnp.zeros((ROWS - 9, CHUNK), F32)
        by_view = [
            jnp.concatenate([r[v : v + 1] for r in records] + [blank], axis=0) for v in range(VIEWS)]
        for b in range(CHUNK // LANES):
            swapped = swap_segments([x[:, b * LANES : (b + 1) * LANES] for x in by_view])
            for o in range(SEGS):
                out_ref[c * (CHUNK // CAP) + b * SEGS + o] = swapped[o][0:FIELDS]

    loop(owners * CAP // CHUNK, project)
    finish = swap_blocks(owners, lambda p: out_ref.at[p], rec_ref, rec_send, rec_recv)
    rec_ref[me] = out_ref[me]

    def selectors(t):
        def part(c):
            at = pl.ds(aligned(c, CHUNK), CHUNK)
            sel_s[t, at, :] = one_hot(c * CHUNK, list_ref[pl.ds(t, 1), :], CHUNK)

        loop(owners * CAP // CHUNK, part)

    loop(list_ref.shape[0], selectors)
    finish()
    raster(
        ids_ref, rec_ref, list_ref, cot_ref, img_ref, out_ref,
        rec_s, sel_s, grad_s, lk_s, alpha_s, ratio_s, shade_s, before_s, w_s, sw_s, swp_s,
    )
    finish = swap_blocks(owners, lambda p: out_ref.at[p], back_ref, back_send, back_recv)
    back_ref[me] = out_ref[me]
    finish()


def pull_kernel(want_ref, back_ref, raw_ref, cam_ref, img_ref, cen_ref, fac_ref, har_ref, opa_ref, out_ref):
    gauss = cen_ref.shape[1]
    out_ref[...] = img_ref[...]
    by_view = [[] for _ in range(VIEWS)]
    for b in range(CHUNK // LANES):
        swapped = swap_segments([back_ref[b * SEGS + o] for o in range(SEGS)])
        for v in range(VIEWS):
            by_view[v].append(swapped[v])
    by_view = [jnp.concatenate(x, axis=1) for x in by_view]
    grads = [jnp.concatenate([by_view[v][c : c + 1] for v in range(VIEWS)], axis=0) for c in range(9)]
    pos, shape, coeffs, logit = raw_rows(raw_ref[...])
    cam = camera_columns(cam_ref)
    (_, basis), pull = jax.vjp(lambda p, s: geometry(p, s, cam), pos, shape)
    basis_grads = []
    for j in range(16):
        total = grads[5] * coeffs[j]
        for c in range(1, 3):
            total = total + grads[5 + c] * coeffs[16 * c + j]
        basis_grads.append(total)
    pos_grads, shape_grads = pull((grads[:5], basis_grads))
    rows = [
        jnp.sum(grads[5 + c] * basis[j], axis=0, keepdims=True) for c in range(3) for j in range(16)
    ]
    rows += list(shape_grads) + list(pos_grads)
    keep = 1.0 - 1.0 / (1.0 + jnp.exp(-logit))
    rows.append(keep * jnp.sum(grads[8], axis=0, keepdims=True))
    rows.append(jnp.zeros((3, CHUNK), F32))
    parts = jnp.concatenate(split(jnp.concatenate(rows, axis=0), 2), axis=0)
    want = want_ref[...]
    first = pl.program_id(0) == 0
    for base in range(0, gauss, CHUNK):
        cols = slice(base, base + CHUNK)
        both = mm_nt(parts, one_hot(base, want, CHUNK))
        total = both[0:64] + both[64:128]

        def put(ref, value):
            @pl.when(first)
            def _():
                ref[:, cols] = value

            @pl.when(jnp.logical_not(first))
            def _():
                ref[:, cols] = ref[:, cols] + value

        put(har_ref, total[0:48])
        put(fac_ref, total[48:57])
        put(cen_ref, total[57:60])
        put(opa_ref, total[60:61])


def loop(count, body):
    if count == 1:
        body(0)
    else:
        def step(i, carry):
            body(i)
            return carry
        lax.fori_loop(0, count, step, 0)


def aligned(i, size):
    return i * size if isinstance(i, int) else pl.multiple_of(i * size, size)


def raster(
    ids_ref, rec_ref, list_ref, cot_ref, img_ref, back_ref,
    rec_s, sel_s, grad_s, lk_s, alpha_s, ratio_s, shade_s, before_s, w_s, sw_s, swp_s,
):
    owners = rec_ref.shape[0]
    slots = owners * CAP
    tiles, length = list_ref.shape
    half = length // 2
    blank = jnp.zeros((ROWS - FIELDS, LANES), F32)

    def unpack(b):
        swapped = swap_segments([rec_ref[b * SEGS + o] for o in range(SEGS)])
        for v in range(VIEWS):
            rec_s[v, :, pl.ds(aligned(b, LANES), LANES)] = jnp.concatenate(
                split(jnp.concatenate([swapped[v], blank], axis=0), 3), axis=0)

    if owners <= 16:
        for b in range(owners // SEGS):
            unpack(b)
    else:
        loop(owners // SEGS, unpack)
    grad_s[...] = jnp.zeros_like(grad_s)

    row_i = lax.broadcasted_iota(jnp.int32, (length, length), 0)
    col_i = lax.broadcasted_iota(jnp.int32, (length, length), 1)
    upper = jnp.where(row_i < col_i, 1.0, 0.0).astype(BF16)
    lower = jnp.where(row_i > col_i, 1.0, 0.0).astype(BF16)
    px = lax.broadcasted_iota(jnp.int32, (TILE, length), 0).astype(F32) + 0.5

    def tile(t, slot):
        code = ids_ref[t]
        view = code // (TILES_ACROSS * TILE_ROWS)
        place = code - view * (TILES_ACROSS * TILE_ROWS)
        line = place // TILES_ACROSS
        corner_y = (line * TILE).astype(F32)
        corner_x = ((place - line * TILES_ACROSS) * TILE).astype(F32)

        def gather(c):
            at = pl.ds(aligned(c, CHUNK), CHUNK)
            return mm(rec_s[view, :, at], sel_s[t, at, :])

        if slots == CHUNK:
            got = gather(0)
        else:
            got = lax.fori_loop(
                0, slots // CHUNK, lambda c, a: a + gather(c), jnp.zeros((3 * ROWS, length), F32))
        rec = got[0:ROWS] + got[ROWS : 2 * ROWS] + got[2 * ROWS :]
        con_a, con_b, con_c = rec[2:3], rec[3:4], rec[4:5]
        colour = rec[5:8]
        strength = rec[8:9]
        dx = (corner_x + px) - rec[0:1]
        dy = (corner_y + px) - rec[1:2]
        quad_x = (-0.5 * LOG2E * con_a) * dx * dx
        cross = (-LOG2E * con_b) * dx
        quad_y = (-0.5 * LOG2E * con_c) * dy * dy
        yield
        for y in range(TILE):
            rows = slice(y * TILE, (y + 1) * TILE)
            falloff = jnp.exp2(quad_x + cross * dy[y : y + 1] + quad_y[y : y + 1])
            alpha = strength * falloff
            keep = jnp.log(1.0 - alpha) * LOG2E
            alpha_s[slot, rows] = alpha
            ratio_s[slot, rows] = alpha * jnp.exp2(-keep)
            hi, lo = split(keep, 2)
            lk_s[slot, 0, rows] = hi
            lk_s[slot, 1, rows] = lo
        yield
        before_s[slot, :, :half] = mm(lk_s[slot, 0, :, :half], upper[:half, :half]) + mm(
            lk_s[slot, 1, :, :half], upper[:half, :half])
        before_s[slot, :, half:] = mm(lk_s[slot, 0], upper[:, half:]) + mm(lk_s[slot, 1], upper[:, half:])

        cot = jnp.concatenate([cot_ref[c, pl.ds(t, 1), :] for c in range(3)], axis=0)
        cot_hi, cot_lo = split(cot, 2)
        col_hi, col_lo = split(colour, 2)
        pad = jnp.zeros((ROWS - 9, PIX), BF16)
        shade_s[slot] = mm_tn(
            jnp.concatenate([cot_hi, cot_hi, cot_lo, pad], axis=0),
            jnp.concatenate([col_hi, col_lo, col_hi, jnp.zeros((ROWS - 9, length), BF16)], axis=0),
        )
        yield
        for y in range(TILE):
            rows = slice(y * TILE, (y + 1) * TILE)
            weight = alpha_s[slot, rows] * jnp.exp2(before_s[slot, rows])
            hi, lo = split(weight, 2)
            w_s[slot, 0, rows] = hi
            w_s[slot, 1, rows] = lo
            shaded = shade_s[slot, rows] * weight
            sw_s[slot, rows] = shaded
            hi, lo = split(shaded, 2)
            swp_s[slot, 0, rows] = hi
            swp_s[slot, 1, rows] = lo
        yield
        before_s[slot, :, half:] = mm(swp_s[slot, 0, :, half:], lower[half:, half:]) + mm(
            swp_s[slot, 1, :, half:], lower[half:, half:])
        before_s[slot, :, :half] = mm(swp_s[slot, 0], lower[:, :half]) + mm(swp_s[slot, 1], lower[:, :half])

        six = jnp.zeros((2, length), BF16)
        col_parts = jnp.concatenate([col_hi, col_lo, six], axis=0)
        by_hi = mm_nt(col_parts, w_s[slot, 0])
        by_lo = mm_nt(col_parts, w_s[slot, 1])
        image = by_hi[0:3] + by_hi[3:6] + by_lo[0:3]
        for c in range(3):
            img_ref[c, pl.ds(t, 1), :] = image[c : c + 1]
        cot_parts = jnp.concatenate([cot_hi, cot_lo, jnp.zeros((2, PIX), BF16)], axis=0)
        by_hi = mm(cot_parts, w_s[slot, 0])
        by_lo = mm(cot_parts, w_s[slot, 1])
        grad_colour = by_hi[0:3] + by_hi[3:6] + by_lo[0:3]

        sum_0 = jnp.zeros((TILE, length), F32)
        sum_1 = jnp.zeros((TILE, length), F32)
        sum_2 = jnp.zeros((TILE, length), F32)
        yield
        for y in range(TILE):
            rows = slice(y * TILE, (y + 1) * TILE)
            g = sw_s[slot, rows] - before_s[slot, rows] * ratio_s[slot, rows]
            g_y = g * dy[y : y + 1]
            sum_0 = sum_0 + g
            sum_1 = sum_1 + g_y
            sum_2 = sum_2 + g_y * dy[y : y + 1]

        yield

        def total(value):
            return jnp.sum(value, axis=0, keepdims=True)

        m_x = sum_0 * dx
        m_0, m_10, m_20 = total(sum_0), total(m_x), total(m_x * dx)
        m_01, m_11, m_02 = total(sum_1), total(sum_1 * dx), total(sum_2)
        back = jnp.concatenate(
            [
                con_a * m_10 + con_b * m_01,
                con_b * m_10 + con_c * m_01,
                -0.5 * m_20,
                -m_11,
                -0.5 * m_02,
                grad_colour,
                m_0,
                jnp.zeros((ROWS - 9, length), F32),
            ],
            axis=0,
        )
        parts = jnp.concatenate(split(back, 2), axis=0)

        def scatter(c):
            at = pl.ds(aligned(c, CHUNK), CHUNK)
            both = mm_nt(parts, sel_s[t, at, :])
            added = both[0:ROWS] + both[ROWS:]
            for v in range(VIEWS):
                grad_s[v, :, at] = grad_s[v, :, at] + jnp.where(view == v, added, 0.0)

        loop(slots // CHUNK, scatter)

    def group(i):
        running = [tile(i * PAIR + slot, slot) for slot in range(PAIR)]
        while running:
            running = [g for g in running if next(g, True) is None]

    loop(tiles // PAIR, group)

    def pack(b):
        swapped = swap_segments([grad_s[v, :, pl.ds(aligned(b, LANES), LANES)] for v in range(VIEWS)])
        for o in range(SEGS):
            back_ref[b * SEGS + o] = swapped[o][0:FIELDS]

    if owners <= 16:
        for b in range(owners // SEGS):
            pack(b)
    else:
        loop(owners // SEGS, pack)


def whole(shape):
    return pl.BlockSpec(shape, lambda i: (0,) * len(shape))


def local(
    centres, factor, harmonics, opacity, cameras, requests, tile_lists, tile_ids, image_cotangent
):
    gauss = centres.shape[1]
    slots = requests.shape[0]
    owners = slots // CAP
    tiles, length = tile_lists.shape
    chunks = slots // CHUNK
    params = pltpu.CompilerParams(vmem_limit_bytes=VMEM_LIMIT)
    want_spec = pl.BlockSpec((1, CHUNK), lambda i: (0, i))
    block_spec = pl.BlockSpec((CHUNK // CAP, FIELDS, LANES), lambda i: (i, 0, 0))
    raw_spec = pl.BlockSpec((64, CHUNK), lambda i: (0, i))
    owned = [whole((3, gauss)), whole((9, gauss)), whole((48, gauss)), whole((1, gauss))]
    block_type = jax.ShapeDtypeStruct((owners, FIELDS, LANES), F32)

    vmem = pl.BlockSpec(memory_space=pltpu.VMEM)
    sems = pltpu.SemaphoreType.DMA((owners,))
    blocks = pltpu.VMEM((owners, FIELDS, LANES), F32)
    plane = pltpu.VMEM((PAIR, PIX, length), F32)
    pair = pltpu.VMEM((PAIR, 2, PIX, length), BF16)
    image_type = jax.ShapeDtypeStruct((3, tiles, PIX), F32)
    image, returned, raw, wanted = pl.pallas_call(
        splat_kernel,
        in_specs=[pl.BlockSpec(memory_space=pl.ANY)] * 9,
        out_specs=[vmem] * 4,
        out_shape=[
            image_type,
            block_type,
            jax.ShapeDtypeStruct((64, slots), F32),
            jax.ShapeDtypeStruct((1, slots), jnp.int32),
        ],
        scratch_shapes=[
            pltpu.VMEM((slots // LANES, 1, LANES), jnp.int32),
            pltpu.VMEM((3, gauss), F32),
            pltpu.VMEM((9, gauss), F32),
            pltpu.VMEM((48, gauss), F32),
            pltpu.VMEM((1, gauss), F32),
            pltpu.VMEM((VIEWS, 3), F32),
            pltpu.SMEM((tiles,), jnp.int32),
            pltpu.VMEM((tiles, length), jnp.int32),
            pltpu.VMEM((3, tiles, PIX), F32),
            pltpu.VMEM((192, gauss), BF16),
            pltpu.VMEM((owners, 1, LANES), jnp.int32),
            pltpu.VMEM((owners, LANES), jnp.int32),
            blocks,
            blocks,
            pltpu.VMEM((VIEWS, 3 * ROWS, slots), BF16),
            pltpu.VMEM((tiles, slots, length), BF16),
            pltpu.VMEM((VIEWS, ROWS, slots), F32),
            pair, plane, plane, plane, plane, pair, plane, pair,
            pltpu.SemaphoreType.DMA((9,)),
            sems, sems, sems, sems, sems, sems,
        ],
        compiler_params=pltpu.CompilerParams(
            vmem_limit_bytes=VMEM_LIMIT, collective_id=0, has_side_effects=True),
    )(
        requests.reshape(slots // LANES, 1, LANES), centres, factor, harmonics,
        opacity.reshape(1, gauss), cameras, tile_ids, tile_lists, image_cotangent,
    )

    grads = pl.pallas_call(
        pull_kernel,
        grid=(chunks,),
        in_specs=[want_spec, block_spec, raw_spec, whole((VIEWS, 3)), whole((3, tiles, PIX))],
        out_specs=owned + [whole((3, tiles, PIX))],
        out_shape=[jax.ShapeDtypeStruct((n, gauss), F32) for n in (3, 9, 48, 1)] + [image_type],
        compiler_params=params,
    )(wanted, returned, raw, cameras, image)
    return (grads[4], grads[0], grads[1], grads[2], grads[3].reshape(gauss))


def solution(mesh):
    in_specs = (
        P(None, ("grp", "gs")),
        P(None, ("grp", "gs")),
        P(None, ("grp", "gs")),
        P(("grp", "gs")),
        P("grp", None),
        P(("grp", "gs")),
        P(("grp", "gs"), None),
        P(("grp", "gs")),
        P(None, ("grp", "gs"), None),
    )
    out_specs = (
        P(None, ("grp", "gs"), None),
        P(None, ("grp", "gs")),
        P(None, ("grp", "gs")),
        P(None, ("grp", "gs")),
        P(("grp", "gs")),
    )
    return jax.shard_map(local, mesh=mesh, in_specs=in_specs, out_specs=out_specs, check_vma=False)
```

```python
import functools

import jax
import jax.numpy as jnp
from jax import lax
from jax.experimental import pallas as pl
from jax.experimental.pallas import tpu as pltpu
from jax.sharding import PartitionSpec as P

TILE = 16
PIX = TILE * TILE
IMG_W = 960
IMG_H = 540
FOCAL = 600
TILES_ACROSS = 60
TILE_ROWS = 33
VIEWS = 4
CAP = 32
LANES = 128
SEGS = LANES // CAP
ROWS = 16
CHUNK = 512
F32 = jnp.float32
BF16 = jnp.bfloat16
VMEM_LIMIT = 60 * 1024 * 1024
FIELDS = 9
PAIR = 4
LOG2E = 1.4426950408889634

BAND_ONE = 0.4886025119029199


def sh_basis(dir_x, dir_y, dir_z):
    sq_x = dir_x * dir_x
    sq_y = dir_y * dir_y
    sq_z = dir_z * dir_z
    return [
        jnp.full_like(dir_x, 0.28209479177387814),
        -BAND_ONE * dir_y,
        BAND_ONE * dir_z,
        -BAND_ONE * dir_x,
        1.0925484305920792 * dir_x * dir_y,
        -1.0925484305920792 * dir_y * dir_z,
        0.31539156525252005 * (2.0 * sq_z - sq_x - sq_y),
        -1.0925484305920792 * dir_x * dir_z,
        0.5462742152960396 * (sq_x - sq_y),
        -0.5900435899266435 * dir_y * (3.0 * sq_x - sq_y),
        2.890611442640554 * dir_x * dir_y * dir_z,
        -0.4570457994644658 * dir_y * (4.0 * sq_z - sq_x - sq_y),
        0.3731763325901154 * dir_z * (2.0 * sq_z - 3.0 * sq_x - 3.0 * sq_y),
        -0.4570457994644658 * dir_x * (4.0 * sq_z - sq_x - sq_y),
        1.445305721320277 * dir_z * (sq_x - sq_y),
        -0.5900435899266435 * dir_x * (sq_x - 3.0 * sq_y),
    ]


def geometry(pos, shape, cam):
    cov = [
        [
            shape[3 * i] * shape[3 * j]
            + shape[3 * i + 1] * shape[3 * j + 1]
            + shape[3 * i + 2] * shape[3 * j + 2]
            for j in range(3)
        ]
        for i in range(3)
    ]
    rel_x = pos[0] - cam[0]
    rel_y = pos[1] - cam[1]
    rel_z = pos[2] - cam[2]
    inverse = 1.0 / rel_z
    screen_x = FOCAL * rel_x * inverse + 0.5 * IMG_W
    screen_y = FOCAL * rel_y * inverse + 0.5 * IMG_H
    jac_xx = FOCAL * inverse
    jac_xz = -FOCAL * rel_x * inverse * inverse
    jac_yz = -FOCAL * rel_y * inverse * inverse
    cov_a = (
        jac_xx * jac_xx * cov[0][0]
        + 2.0 * jac_xx * jac_xz * cov[0][2]
        + jac_xz * jac_xz * cov[2][2]
        + 0.3
    )
    cov_b = (
        jac_xx * jac_xx * cov[0][1]
        + jac_xx * jac_yz * cov[0][2]
        + jac_xz * jac_xx * cov[2][1]
        + jac_xz * jac_yz * cov[2][2]
    )
    cov_c = (
        jac_xx * jac_xx * cov[1][1]
        + 2.0 * jac_xx * jac_yz * cov[1][2]
        + jac_yz * jac_yz * cov[2][2]
        + 0.3
    )
    scale = 1.0 / (cov_a * cov_c - cov_b * cov_b)
    shrink = 1.0 / jnp.sqrt(rel_x * rel_x + rel_y * rel_y + rel_z * rel_z)
    basis = sh_basis(rel_x * shrink, rel_y * shrink, rel_z * shrink)
    return [screen_x, screen_y, cov_c * scale, -cov_b * scale, cov_a * scale], basis


def split(value, parts):
    out = []
    for _ in range(parts - 1):
        piece = value.astype(BF16)
        out.append(piece)
        value = value - piece.astype(F32)
    out.append(value.astype(BF16))
    return out


def mm(a, b):
    return jnp.dot(a, b, preferred_element_type=F32)


def mm_nt(a, b):
    return lax.dot_general(a, b, (((1,), (1,)), ((), ())), preferred_element_type=F32)


def mm_tn(a, b):
    return lax.dot_general(a, b, (((0,), (0,)), ((), ())), preferred_element_type=F32)


def swap_segments(arrays):
    seg = lax.broadcasted_iota(jnp.int32, arrays[0].shape, 1) // CAP
    turned = [[a if s == 0 else pltpu.roll(a, CAP * s, 1) for s in range(SEGS)] for a in arrays]
    out = []
    for o in range(SEGS):
        z = turned[0][(0 - o) % SEGS]
        for v in range(1, SEGS):
            z = jnp.where(seg == v, turned[v][(v - o) % SEGS], z)
        out.append(z)
    return out


def one_hot(base, index, rows):
    ids = lax.broadcasted_iota(jnp.int32, (rows, index.shape[1]), 0) + base
    return jnp.where(ids == index, 1.0, 0.0).astype(BF16)


def raw_rows(raw):
    def row(i):
        return raw[i : i + 1]
    return (
        [row(57 + i) for i in range(3)],
        [row(48 + i) for i in range(9)],
        [row(i) for i in range(48)],
        row(60),
    )


def camera_columns(cam_ref):
    return [cam_ref[:, i : i + 1] for i in range(3)]


def partners(owners, body):
    me = lax.axis_index("gs")

    def step(i, carry):
        body(lax.rem(me + i, owners))
        return carry

    lax.fori_loop(1, owners, step, 0, unroll=owners <= 16)


def greet(owners):
    barrier = pltpu.get_barrier_semaphore()
    partners(owners, lambda p: pl.semaphore_signal(
        barrier, inc=1, device_id={"gs": p}, device_id_type=pl.DeviceIdType.MESH))
    return barrier


def block_copy(source, target, send_sem, recv_sem, sender, partner):
    return pltpu.make_async_remote_copy(
        src_ref=source, dst_ref=target, send_sem=send_sem.at[partner], recv_sem=recv_sem.at[sender],
        device_id={"gs": partner}, device_id_type=pl.DeviceIdType.MESH)


def swap_blocks(owners, source, target, send_sem, recv_sem):
    me = lax.axis_index("gs")
    partners(owners, lambda p: block_copy(
        source(p), target.at[me], send_sem, recv_sem, me, p).start())

    def finish():
        partners(owners, lambda p: block_copy(
            source(p), target.at[p], send_sem, recv_sem, p, p).wait_recv())
        partners(owners, lambda p: block_copy(
            source(p), target.at[me], send_sem, recv_sem, me, p).wait_send())

    return finish


def splat_kernel(
    req_hbm, cen_hbm, fac_hbm, har_hbm, opa_hbm, cam_hbm, ids_hbm, list_hbm, cot_hbm,
    img_ref, back_ref, raw_ref, want_ref,
    req_ref, cen_ref, fac_ref, har_ref, opa_ref, cam_ref, ids_ref, list_ref, cot_ref,
    parts_ref, got_ref, ask_ref, out_ref, rec_ref,
    rec_s, sel_s, grad_s, lk_s, alpha_s, ratio_s, shade_s, before_s, w_s, sw_s, swp_s,
    load_sem, ask_send, ask_recv, rec_send, rec_recv, back_send, back_recv,
):
    owners = rec_ref.shape[0]
    gauss = cen_ref.shape[1]
    me = lax.axis_index("gs")
    loads = [
        pltpu.make_async_copy(src, dst, load_sem.at[i])
        for i, (src, dst) in enumerate([
            (req_hbm, req_ref), (har_hbm, har_ref), (fac_hbm, fac_ref), (cen_hbm, cen_ref),
            (opa_hbm, opa_ref), (cam_hbm, cam_ref), (ids_hbm, ids_ref), (list_hbm, list_ref),
            (cot_hbm, cot_ref)])
    ]
    for load in loads:
        load.start()
    barrier = greet(owners)
    loads[0].wait()
    pl.semaphore_wait(barrier, owners - 1)
    finish = swap_blocks(owners, lambda p: req_ref.at[p // SEGS], got_ref, ask_send, ask_recv)
    got_ref[me] = req_ref[me // SEGS]
    for load in loads[1:]:
        load.wait()
    for base in range(0, gauss, CHUNK):
        cols = slice(base, base + CHUNK)
        whole = jnp.concatenate(
            [har_ref[:, cols], fac_ref[:, cols], cen_ref[:, cols], opa_ref[:, cols],
             jnp.zeros((3, CHUNK), F32)], axis=0)
        parts_ref[:, cols] = jnp.concatenate(split(whole, 3), axis=0)
    finish()
    seg = lax.broadcasted_iota(jnp.int32, (owners, LANES), 1) // CAP
    row = lax.broadcasted_iota(jnp.int32, (owners, LANES), 0)
    mine = jnp.where(seg == lax.rem(me, SEGS), got_ref[:, 0, :], 0)
    spread = mine
    for s in range(1, SEGS):
        spread = spread + pltpu.roll(mine, CAP * s, 1)
    ask_ref[...] = jnp.where(seg == lax.rem(row, SEGS), spread, 0)

    def project(c):
        near = ask_ref[pl.ds(aligned(c, CHUNK // CAP), CHUNK // CAP), :]
        asked = jnp.concatenate(
            [jnp.sum(near[b * SEGS : (b + 1) * SEGS], axis=0, keepdims=True)
             for b in range(CHUNK // LANES)], axis=1)
        lanes = pl.ds(aligned(c, CHUNK), CHUNK)
        want_ref[:, lanes] = asked
        want = jnp.maximum(asked, 0)
        acc = jnp.zeros((192, CHUNK), F32)
        for base in range(0, gauss, CHUNK):
            acc = acc + mm(parts_ref[:, base : base + CHUNK], one_hot(base, want, CHUNK))
        raw = acc[0:64] + acc[64:128] + acc[128:192]
        raw_ref[:, lanes] = raw
        pos, shape, coeffs, logit = raw_rows(raw)
        records, basis = geometry(pos, shape, camera_columns(cam_ref))
        for ch in range(3):
            summed = jnp.full_like(basis[0], 0.5)
            for j in range(16):
                summed = summed + basis[j] * coeffs[16 * ch + j]
            records.append(summed)
        strength = 1.0 / (1.0 + jnp.exp(-logit))
        records.append(jnp.broadcast_to(strength, (VIEWS, CHUNK)))
        blank = jnp.zeros((ROWS - 9, CHUNK), F32)
        by_view = [
            jnp.concatenate([r[v : v + 1] for r in records] + [blank], axis=0) for v in range(VIEWS)]
        for b in range(CHUNK // LANES):
            swapped = swap_segments([x[:, b * LANES : (b + 1) * LANES] for x in by_view])
            for o in range(SEGS):
                out_ref[c * (CHUNK // CAP) + b * SEGS + o] = swapped[o][0:FIELDS]

    loop(owners * CAP // CHUNK, project)
    finish = swap_blocks(owners, lambda p: out_ref.at[p], rec_ref, rec_send, rec_recv)
    rec_ref[me] = out_ref[me]

    def selectors(t):
        def part(c):
            at = pl.ds(aligned(c, CHUNK), CHUNK)
            sel_s[t, at, :] = one_hot(c * CHUNK, list_ref[pl.ds(t, 1), :], CHUNK)

        loop(owners * CAP // CHUNK, part)

    loop(list_ref.shape[0], selectors)
    finish()
    raster(
        ids_ref, rec_ref, list_ref, cot_ref, img_ref, out_ref,
        rec_s, sel_s, grad_s, lk_s, alpha_s, ratio_s, shade_s, before_s, w_s, sw_s, swp_s,
    )
    finish = swap_blocks(owners, lambda p: out_ref.at[p], back_ref, back_send, back_recv)
    back_ref[me] = out_ref[me]
    finish()


def pull_kernel(want_ref, back_ref, raw_ref, cam_ref, img_ref, cen_ref, fac_ref, har_ref, opa_ref, out_ref):
    gauss = cen_ref.shape[1]
    out_ref[...] = img_ref[...]
    by_view = [[] for _ in range(VIEWS)]
    for b in range(CHUNK // LANES):
        swapped = swap_segments([back_ref[b * SEGS + o] for o in range(SEGS)])
        for v in range(VIEWS):
            by_view[v].append(swapped[v])
    by_view = [jnp.concatenate(x, axis=1) for x in by_view]
    grads = [jnp.concatenate([by_view[v][c : c + 1] for v in range(VIEWS)], axis=0) for c in range(9)]
    pos, shape, coeffs, logit = raw_rows(raw_ref[...])
    cam = camera_columns(cam_ref)
    (_, basis), pull = jax.vjp(lambda p, s: geometry(p, s, cam), pos, shape)
    basis_grads = []
    for j in range(16):
        total = grads[5] * coeffs[j]
        for c in range(1, 3):
            total = total + grads[5 + c] * coeffs[16 * c + j]
        basis_grads.append(total)
    pos_grads, shape_grads = pull((grads[:5], basis_grads))
    rows = [
        jnp.sum(grads[5 + c] * basis[j], axis=0, keepdims=True) for c in range(3) for j in range(16)
    ]
    rows += list(shape_grads) + list(pos_grads)
    keep = 1.0 - 1.0 / (1.0 + jnp.exp(-logit))
    rows.append(keep * jnp.sum(grads[8], axis=0, keepdims=True))
    rows.append(jnp.zeros((3, CHUNK), F32))
    parts = jnp.concatenate(split(jnp.concatenate(rows, axis=0), 2), axis=0)
    want = want_ref[...]
    first = pl.program_id(0) == 0
    for base in range(0, gauss, CHUNK):
        cols = slice(base, base + CHUNK)
        both = mm_nt(parts, one_hot(base, want, CHUNK))
        total = both[0:64] + both[64:128]

        def put(ref, value):
            @pl.when(first)
            def _():
                ref[:, cols] = value

            @pl.when(jnp.logical_not(first))
            def _():
                ref[:, cols] = ref[:, cols] + value

        put(har_ref, total[0:48])
        put(fac_ref, total[48:57])
        put(cen_ref, total[57:60])
        put(opa_ref, total[60:61])


def loop(count, body):
    if count == 1:
        body(0)
    else:
        def step(i, carry):
            body(i)
            return carry
        lax.fori_loop(0, count, step, 0)


def aligned(i, size):
    return i * size if isinstance(i, int) else pl.multiple_of(i * size, size)


def raster(
    ids_ref, rec_ref, list_ref, cot_ref, img_ref, back_ref,
    rec_s, sel_s, grad_s, lk_s, alpha_s, ratio_s, shade_s, before_s, w_s, sw_s, swp_s,
):
    owners = rec_ref.shape[0]
    slots = owners * CAP
    tiles, length = list_ref.shape
    half = length // 2
    blank = jnp.zeros((ROWS - FIELDS, LANES), F32)

    def unpack(b):
        swapped = swap_segments([rec_ref[b * SEGS + o] for o in range(SEGS)])
        for v in range(VIEWS):
            rec_s[v, :, pl.ds(aligned(b, LANES), LANES)] = jnp.concatenate(
                split(jnp.concatenate([swapped[v], blank], axis=0), 3), axis=0)

    if owners <= 16:
        for b in range(owners // SEGS):
            unpack(b)
    else:
        loop(owners // SEGS, unpack)
    grad_s[...] = jnp.zeros_like(grad_s)

    row_i = lax.broadcasted_iota(jnp.int32, (length, length), 0)
    col_i = lax.broadcasted_iota(jnp.int32, (length, length), 1)
    upper = jnp.where(row_i < col_i, 1.0, 0.0).astype(BF16)
    lower = jnp.where(row_i > col_i, 1.0, 0.0).astype(BF16)
    px = lax.broadcasted_iota(jnp.int32, (TILE, length), 0).astype(F32) + 0.5

    def tile(t, slot):
        code = ids_ref[t]
        view = code // (TILES_ACROSS * TILE_ROWS)
        place = code - view * (TILES_ACROSS * TILE_ROWS)
        line = place // TILES_ACROSS
        corner_y = (line * TILE).astype(F32)
        corner_x = ((place - line * TILES_ACROSS) * TILE).astype(F32)

        def gather(c):
            at = pl.ds(aligned(c, CHUNK), CHUNK)
            return mm(rec_s[view, :, at], sel_s[t, at, :])

        if slots == CHUNK:
            got = gather(0)
        else:
            got = lax.fori_loop(
                0, slots // CHUNK, lambda c, a: a + gather(c), jnp.zeros((3 * ROWS, length), F32))
        rec = got[0:ROWS] + got[ROWS : 2 * ROWS] + got[2 * ROWS :]
        con_a, con_b, con_c = rec[2:3], rec[3:4], rec[4:5]
        colour = rec[5:8]
        strength = rec[8:9]
        dx = (corner_x + px) - rec[0:1]
        dy = (corner_y + px) - rec[1:2]
        quad_x = (-0.5 * LOG2E * con_a) * dx * dx
        cross = (-LOG2E * con_b) * dx
        quad_y = (-0.5 * LOG2E * con_c) * dy * dy
        yield
        for y in range(TILE):
            rows = slice(y * TILE, (y + 1) * TILE)
            falloff = jnp.exp2(quad_x + cross * dy[y : y + 1] + quad_y[y : y + 1])
            alpha = strength * falloff
            keep = jnp.log(1.0 - alpha) * LOG2E
            alpha_s[slot, rows] = alpha
            ratio_s[slot, rows] = alpha * jnp.exp2(-keep)
            hi, lo = split(keep, 2)
            lk_s[slot, 0, rows] = hi
            lk_s[slot, 1, rows] = lo
        yield
        before_s[slot, :, :half] = mm(lk_s[slot, 0, :, :half], upper[:half, :half]) + mm(
            lk_s[slot, 1, :, :half], upper[:half, :half])
        before_s[slot, :, half:] = mm(lk_s[slot, 0], upper[:, half:]) + mm(lk_s[slot, 1], upper[:, half:])

        cot = jnp.concatenate([cot_ref[c, pl.ds(t, 1), :] for c in range(3)], axis=0)
        cot_hi, cot_lo = split(cot, 2)
        col_hi, col_lo = split(colour, 2)
        pad = jnp.zeros((ROWS - 9, PIX), BF16)
        shade_s[slot] = mm_tn(
            jnp.concatenate([cot_hi, cot_hi, cot_lo, pad], axis=0),
            jnp.concatenate([col_hi, col_lo, col_hi, jnp.zeros((ROWS - 9, length), BF16)], axis=0),
        )
        yield
        for y in range(TILE):
            rows = slice(y * TILE, (y + 1) * TILE)
            weight = alpha_s[slot, rows] * jnp.exp2(before_s[slot, rows])
            hi, lo = split(weight, 2)
            w_s[slot, 0, rows] = hi
            w_s[slot, 1, rows] = lo
            shaded = shade_s[slot, rows] * weight
            sw_s[slot, rows] = shaded
            hi, lo = split(shaded, 2)
            swp_s[slot, 0, rows] = hi
            swp_s[slot, 1, rows] = lo
        yield
        before_s[slot, :, half:] = mm(swp_s[slot, 0, :, half:], lower[half:, half:]) + mm(
            swp_s[slot, 1, :, half:], lower[half:, half:])
        before_s[slot, :, :half] = mm(swp_s[slot, 0], lower[:, :half]) + mm(swp_s[slot, 1], lower[:, :half])

        six = jnp.zeros((2, length), BF16)
        col_parts = jnp.concatenate([col_hi, col_lo, six], axis=0)
        by_hi = mm_nt(col_parts, w_s[slot, 0])
        by_lo = mm_nt(col_parts, w_s[slot, 1])
        image = by_hi[0:3] + by_hi[3:6] + by_lo[0:3]
        for c in range(3):
            img_ref[c, pl.ds(t, 1), :] = image[c : c + 1]
        cot_parts = jnp.concatenate([cot_hi, cot_lo, jnp.zeros((2, PIX), BF16)], axis=0)
        by_hi = mm(cot_parts, w_s[slot, 0])
        by_lo = mm(cot_parts, w_s[slot, 1])
        grad_colour = by_hi[0:3] + by_hi[3:6] + by_lo[0:3]

        sum_0 = jnp.zeros((TILE, length), F32)
        sum_1 = jnp.zeros((TILE, length), F32)
        sum_2 = jnp.zeros((TILE, length), F32)
        yield
        for y in range(TILE):
            rows = slice(y * TILE, (y + 1) * TILE)
            g = sw_s[slot, rows] - before_s[slot, rows] * ratio_s[slot, rows]
            g_y = g * dy[y : y + 1]
            sum_0 = sum_0 + g
            sum_1 = sum_1 + g_y
            sum_2 = sum_2 + g_y * dy[y : y + 1]

        yield

        def total(value):
            return jnp.sum(value, axis=0, keepdims=True)

        m_x = sum_0 * dx
        m_0, m_10, m_20 = total(sum_0), total(m_x), total(m_x * dx)
        m_01, m_11, m_02 = total(sum_1), total(sum_1 * dx), total(sum_2)
        back = jnp.concatenate(
            [
                con_a * m_10 + con_b * m_01,
                con_b * m_10 + con_c * m_01,
                -0.5 * m_20,
                -m_11,
                -0.5 * m_02,
                grad_colour,
                m_0,
                jnp.zeros((ROWS - 9, length), F32),
            ],
            axis=0,
        )
        parts = jnp.concatenate(split(back, 2), axis=0)

        def scatter(c):
            at = pl.ds(aligned(c, CHUNK), CHUNK)
            both = mm_nt(parts, sel_s[t, at, :])
            added = both[0:ROWS] + both[ROWS:]
            for v in range(VIEWS):
                grad_s[v, :, at] = grad_s[v, :, at] + jnp.where(view == v, added, 0.0)

        loop(slots // CHUNK, scatter)

    def group(i):
        running = [tile(i * PAIR + slot, slot) for slot in range(PAIR)]
        while running:
            running = [g for g in running if next(g, True) is None]

    loop(tiles // PAIR, group)

    def pack(b):
        swapped = swap_segments([grad_s[v, :, pl.ds(aligned(b, LANES), LANES)] for v in range(VIEWS)])
        for o in range(SEGS):
            back_ref[b * SEGS + o] = swapped[o][0:FIELDS]

    if owners <= 16:
        for b in range(owners // SEGS):
            pack(b)
    else:
        loop(owners // SEGS, pack)


def whole(shape):
    return pl.BlockSpec(shape, lambda i: (0,) * len(shape))


def local(
    centres, factor, harmonics, opacity, cameras, requests, tile_lists, tile_ids, image_cotangent
):
    gauss = centres.shape[1]
    slots = requests.shape[0]
    owners = slots // CAP
    tiles, length = tile_lists.shape
    chunks = slots // CHUNK
    params = pltpu.CompilerParams(vmem_limit_bytes=VMEM_LIMIT)
    want_spec = pl.BlockSpec((1, CHUNK), lambda i: (0, i))
    block_spec = pl.BlockSpec((CHUNK // CAP, FIELDS, LANES), lambda i: (i, 0, 0))
    raw_spec = pl.BlockSpec((64, CHUNK), lambda i: (0, i))
    owned = [whole((3, gauss)), whole((9, gauss)), whole((48, gauss)), whole((1, gauss))]
    block_type = jax.ShapeDtypeStruct((owners, FIELDS, LANES), F32)

    vmem = pl.BlockSpec(memory_space=pltpu.VMEM)
    sems = pltpu.SemaphoreType.DMA((owners,))
    blocks = pltpu.VMEM((owners, FIELDS, LANES), F32)
    plane = pltpu.VMEM((PAIR, PIX, length), F32)
    pair = pltpu.VMEM((PAIR, 2, PIX, length), BF16)
    image_type = jax.ShapeDtypeStruct((3, tiles, PIX), F32)
    image, returned, raw, wanted = pl.pallas_call(
        splat_kernel,
        in_specs=[pl.BlockSpec(memory_space=pl.ANY)] * 9,
        out_specs=[vmem] * 4,
        out_shape=[
            image_type,
            block_type,
            jax.ShapeDtypeStruct((64, slots), F32),
            jax.ShapeDtypeStruct((1, slots), jnp.int32),
        ],
        scratch_shapes=[
            pltpu.VMEM((slots // LANES, 1, LANES), jnp.int32),
            pltpu.VMEM((3, gauss), F32),
            pltpu.VMEM((9, gauss), F32),
            pltpu.VMEM((48, gauss), F32),
            pltpu.VMEM((1, gauss), F32),
            pltpu.VMEM((VIEWS, 3), F32),
            pltpu.SMEM((tiles,), jnp.int32),
            pltpu.VMEM((tiles, length), jnp.int32),
            pltpu.VMEM((3, tiles, PIX), F32),
            pltpu.VMEM((192, gauss), BF16),
            pltpu.VMEM((owners, 1, LANES), jnp.int32),
            pltpu.VMEM((owners, LANES), jnp.int32),
            blocks,
            blocks,
            pltpu.VMEM((VIEWS, 3 * ROWS, slots), BF16),
            pltpu.VMEM((tiles, slots, length), BF16),
            pltpu.VMEM((VIEWS, ROWS, slots), F32),
            pair, plane, plane, plane, plane, pair, plane, pair,
            pltpu.SemaphoreType.DMA((9,)),
            sems, sems, sems, sems, sems, sems,
        ],
        compiler_params=pltpu.CompilerParams(
            vmem_limit_bytes=VMEM_LIMIT, collective_id=0, has_side_effects=True),
    )(
        requests.reshape(slots // LANES, 1, LANES), centres, factor, harmonics,
        opacity.reshape(1, gauss), cameras, tile_ids, tile_lists, image_cotangent,
    )

    grads = pl.pallas_call(
        pull_kernel,
        grid=(chunks,),
        in_specs=[want_spec, block_spec, raw_spec, whole((VIEWS, 3)), whole((3, tiles, PIX))],
        out_specs=owned + [whole((3, tiles, PIX))],
        out_shape=[jax.ShapeDtypeStruct((n, gauss), F32) for n in (3, 9, 48, 1)] + [image_type],
        compiler_params=params,
    )(wanted, returned, raw, cameras, image)
    return (grads[4], grads[0], grads[1], grads[2], grads[3].reshape(gauss))


def solution(mesh):
    in_specs = (
        P(None, ("grp", "gs")),
        P(None, ("grp", "gs")),
        P(None, ("grp", "gs")),
        P(("grp", "gs")),
        P("grp", None),
        P(("grp", "gs")),
        P(("grp", "gs"), None),
        P(("grp", "gs")),
        P(None, ("grp", "gs"), None),
    )
    out_specs = (
        P(None, ("grp", "gs"), None),
        P(None, ("grp", "gs")),
        P(None, ("grp", "gs")),
        P(None, ("grp", "gs")),
        P(("grp", "gs")),
    )
    return jax.shard_map(local, mesh=mesh, in_specs=in_specs, out_specs=out_specs, check_vma=False)
```
